512 devices in a mesh: expert: 64 (over z, y), context: 4 (over x), pipe: 2 (over core).
Axes of the slice: x: 4, y: 4, z: 16, core: 2. Of those that a mesh axis runs over, the one named last changes fastest.
Arguments:
- hidden_in: bfloat16 [448, 3584], P('expert'), may hold values from -6 to 6
- draft_embeds: bfloat16 [2, 448, 3584], P(None, 'expert'), may hold values from -6 to 6
- norm_gains: float32 [2, 3584], replicated, may hold values from 0.1 to 1.9
- queries: bfloat16 [2, 448, 64, 576], P(None, 'expert'), may hold values from -72 to 72
- latent_cache: bfloat16 [448, 1024, 576], P('expert', ('context', 'pipe')), may hold values from -6 to 6
- lengths: int32 [448], P('expert'), may hold values from 2 to 1024, as said below
- route_ids: int32 [2, 448, 8], P(None, 'expert'), may hold values from 0 to 63, all different within a row; in each aligned block of 7 rows (0 to 6, 7 to 13, ..., all dimensions but the last counted through in order) at most 2 rows name the same one
- route_weights: float32 [2, 448, 8], P(None, 'expert'), may hold values from 0.1 to 0.6
- w_gate: bfloat16 [64, 3584, 1024], P('expert', None, ('context', 'pipe')), may hold values from -0.09375 to 0.09375
- w_up: bfloat16 [64, 3584, 1024], P('expert', None, ('context', 'pipe')), may hold values from -0.09375 to 0.09375
- w_down: bfloat16 [64, 1024, 3584], P('expert', ('context', 'pipe')), may hold values from -0.1875 to 0.1875
Outputs:
- attended: bfloat16 [2, 448, 64, 512], P(None, 'expert', ('context', 'pipe'))
- hidden_out: bfloat16 [448, 3584], P('expert')
The draws below stay inside these ranges and needn't reach their ends.
Inputs may be any that keep to these rules, and one draw needn't show every extreme that they name: `route_ids`: each row names 8 different experts. Among the 7 rows of one index of expert in one step, no expert is named by more than 2 rows, a bound that some block reaches. `lengths`: some row has all 1024 positions live in every draw.
All inputs are finite; a program needn't handle non-finite values.
Results may differ from the reference program's by a relative error of at most 0.024.
Values may be sent and summed in bfloat16 or wider, within the bound.
A program may use at most 128 MiB of HBM per device.

```python
import math
import jax
import jax.numpy as jnp
import numpy as np
from jax import lax

D = 3584
HEADS = 64
LATENT = 512
KDIM = 576
FE = 1024
EXPERTS = 64
TOPK = 8
CAP = 2
RDEV = 7
LOOPS = 2
CTX = 1024
ROWS = 448
N_EXPERT = 64


def shared_draws(key):
    base_key = jax.random.fold_in(key, 0)
    base = jnp.clip(jax.random.normal(base_key, (ROWS, CTX, KDIM), jnp.float32), -6.0, 6.0)
    return base


def draw_latent_cache(key, part):
    base = shared_draws(key)
    return base.astype(jnp.bfloat16)


def draw_queries(key, part):
    key = jax.random.fold_in(key, 13)
    noise_key = jax.random.fold_in(key, 0)
    values = jnp.clip(jax.random.normal(noise_key, (LOOPS, ROWS, HEADS, KDIM), jnp.float32), -6.0, 6.0)
    return values.astype(jnp.bfloat16)


def draw_lengths(key, part):
    key = jax.random.fold_in(key, 17)
    drawn = jax.random.randint(key, (ROWS,), 2, CTX + 1, jnp.int32)
    return drawn.at[0].set(CTX)


def block_scale(stream_key, extent, shards, smallest, top_value):
    level, own = 1.0, jax.random.fold_in(stream_key, 6)
    for axis_at, parts in shards:
        heights = jnp.exp(jax.random.uniform(jax.random.fold_in(own, axis_at), (parts,), jnp.float32, smallest / len(shards), top_value / len(shards)))
        level = level * jnp.repeat(heights, extent[axis_at] // parts).reshape([-1 if axis == axis_at else 1 for axis in range(len(extent))])
    return level


def assign_block(key, own, number, rows, count, top, limit, slope):
    sequence = jax.random.permutation(key, count)
    heavy_load, usual = load_shares(count, rows * top, limit, slope, True), load_shares(count, rows * top, limit, slope, False)
    places = jnp.arange(count)

    def named(tallies, turn):
        used = int((tallies > 0).sum())
        fixed = max(1, used // 4)
        moved = fixed + (places - fixed + turn * (used - fixed)) % max(1, count - fixed)
        return jnp.zeros((count,), jnp.int32).at[sequence[jnp.where(places < fixed, places, moved)]].set(jnp.asarray(tallies, jnp.int32))

    tallies = jnp.where(number % 4 == 0, named(heavy_load, number // 4), named(usual, number - number // 4 - 1))
    mixed = jax.random.permutation(jax.random.fold_in(own, 3), count)
    donor, receiver = mixed[0:count // 2 * 2:2], mixed[1:count // 2 * 2:2]
    margin = jnp.minimum(tallies[donor] - 1, limit - tallies[receiver]) // 2
    margin = jnp.where((donor == sequence[0]) | (receiver == sequence[0]) | (tallies[receiver] == 0), 0, jnp.maximum(margin, 0))
    moved = jax.random.randint(jax.random.fold_in(own, 4), (count // 2,), 0, 1 << 20) % (margin + 1)
    tallies = tallies.at[donor].add(-moved).at[receiver].add(moved)
    items = jnp.searchsorted(jnp.cumsum(tallies), jnp.arange(rows * top), side="right").astype(jnp.int32)
    listing = items.reshape(top, rows).T
    listing = listing[jax.random.permutation(jax.random.fold_in(own, 1), rows)]
    turn = jax.random.randint(jax.random.fold_in(own, 2), (rows, 1), 0, top)
    return jnp.take_along_axis(listing, (jnp.arange(top)[None, :] + turn) % top, axis=1)


def load_shares(number_of, total, bound, lean, full):
    loads = [(1 << 20) // math.isqrt(rank ** lean) + 1 for rank in range(1, number_of + 1)]
    largest = bound if full else min(bound, max(-(-total // number_of), total * loads[0] // sum(loads)))
    least = 1 if total - largest >= number_of - 1 else 0
    given, surplus = [largest] + [least] * (number_of - 1), total - largest - least * (number_of - 1)
    while surplus > 0:
        free = [i for i in range(1, number_of) if given[i] < largest] or [i for i in range(1, number_of) if given[i] < bound]
        whole, left = sum([loads[i] for i in free]), surplus
        for i in free:
            addition = min(bound - given[i], max(1, left * loads[i] // whole), surplus)
            given[i] = given[i] + addition
            surplus = surplus - addition
    return np.array(given)


def gaussian(own_key, extent, scale, most, shards=(), kind=jnp.bfloat16):
    level = block_scale(own_key, extent, shards, -0.22, 0.18) if shards else 1.0
    values = jax.random.normal(own_key, extent, jnp.float32) * scale * level
    return jnp.minimum(jnp.maximum(values, -most), most).astype(kind)


def setup_inputs(seed: int = 0) -> dict:
    arg_keys = jax.random.split(jax.random.key(seed), 12)
    hidden_in = gaussian(arg_keys[0], (ROWS, D), 1.0, 6.0, ((0, 64),))
    draft_embeds = gaussian(arg_keys[1], (LOOPS, ROWS, D), 1.0, 6.0, ((1, 64),))
    norm_gains = jnp.clip(1.0 + 0.18 * jax.random.normal(arg_keys[2], (2, D), jnp.float32), 0.1, 1.9)
    queries = draw_queries(jax.random.fold_in(arg_keys[11], 71), 0)
    latent_cache = draw_latent_cache(jax.random.fold_in(arg_keys[11], 71), 0)
    lengths = draw_lengths(jax.random.fold_in(arg_keys[11], 71), 0)
    route_ids_keys = jax.random.split(jax.random.fold_in(arg_keys[6], 1), LOOPS * ROWS // RDEV)
    route_ids_turns = jax.random.permutation(jax.random.fold_in(arg_keys[6], 3), LOOPS * ROWS // RDEV)
    route_ids = jax.vmap(lambda own, number: assign_block(jax.random.fold_in(arg_keys[6], 2), own, number, RDEV, EXPERTS, TOPK, CAP, 2))(route_ids_keys, route_ids_turns).reshape((LOOPS, ROWS, TOPK))
    route_weights = jnp.clip(0.1 + 0.5 * jax.random.uniform(arg_keys[7], (LOOPS, ROWS, TOPK), jnp.float32) ** block_scale(arg_keys[7], (LOOPS, ROWS, TOPK), ((1, 64),), -0.2, 0.2), 0.1, 0.6)
    w_gate = gaussian(arg_keys[8], (EXPERTS, D, FE), D ** -0.5, 0.09375, ((0, 64), (2, 8)))
    w_up = gaussian(arg_keys[9], (EXPERTS, D, FE), D ** -0.5, 0.09375, ((0, 64), (2, 8)))
    w_down = gaussian(arg_keys[10], (EXPERTS, FE, D), FE ** -0.5, 0.1875, ((0, 64), (1, 8)))
    return dict(hidden_in=hidden_in, draft_embeds=draft_embeds, norm_gains=norm_gains, queries=queries, latent_cache=latent_cache, lengths=lengths, route_ids=route_ids, route_weights=route_weights, w_gate=w_gate, w_up=w_up, w_down=w_down)


EPSILON = 1e-06
NEG_FILL = -1e+30

def normalize(values, gain):
    values = values.astype(jnp.float32)
    return values * lax.rsqrt(lax.optimization_barrier(jnp.mean(values * values, axis=-1, keepdims=True)) + EPSILON) * gain

def expert_apply(packed):
    rows_in, gate_mat, up_mat, down_mat = packed
    gate_out = jnp.dot(rows_in, gate_mat, preferred_element_type=jnp.float32)
    up_out = jnp.dot(rows_in, up_mat, preferred_element_type=jnp.float32)
    active = (jax.nn.silu(gate_out) * up_out).astype(jnp.bfloat16)
    return jnp.dot(active, down_mat, preferred_element_type=jnp.float32)

def reference(hidden_in, draft_embeds, norm_gains, queries, latent_cache, lengths, route_ids, route_weights, w_gate, w_up, w_down):
    scale_factor = float(KDIM) ** (-0.5)
    positions = jnp.arange(CTX, dtype=jnp.int32)
    visible = positions[None, :] < lengths[:, None]
    cache_wide = latent_cache.astype(jnp.float32)
    values_wide = cache_wide[:, :, :LATENT]
    hidden = hidden_in
    results = []
    for loop_index in range(LOOPS):
        scores = jnp.einsum('rhc,rtc->rht', queries[loop_index].astype(jnp.float32), cache_wide) * scale_factor
        scores = jnp.where(visible[:, None, :], scores, NEG_FILL)
        largest = lax.optimization_barrier(jnp.max(scores, axis=-1, keepdims=True))
        weights = jnp.where(visible[:, None, :], jnp.exp(scores - largest), 0.0).astype(jnp.bfloat16)
        total = lax.optimization_barrier(jnp.sum(weights.astype(jnp.float32), axis=-1))
        summed = jnp.einsum('rht,rtl->rhl', weights.astype(jnp.float32), values_wide)
        results.append((summed / total[..., None]).astype(jnp.bfloat16))
        mixed = normalize(hidden, norm_gains[0]) + normalize(draft_embeds[loop_index], norm_gains[1])
        mixed_low = mixed.astype(jnp.bfloat16)
        chosen_ids = route_ids[loop_index]
        onehot = (chosen_ids[:, :, None] == jnp.arange(EXPERTS, dtype=jnp.int32)[None, None, :]).astype(jnp.int32)
        chosen = lax.optimization_barrier(jnp.sum(onehot, axis=1)).reshape(N_EXPERT, RDEV, EXPERTS)
        earlier = (jnp.cumsum(chosen, axis=1) - chosen).reshape(ROWS, EXPERTS)
        slot_index = jnp.take_along_axis(earlier, chosen_ids, axis=1)
        source = (jnp.arange(ROWS, dtype=jnp.int32) // RDEV)[:, None]
        target = (source * CAP + slot_index).astype(jnp.int32)
        buffer = jnp.zeros((EXPERTS, N_EXPERT * CAP, D), jnp.bfloat16)
        buffer = buffer.at[chosen_ids, target].set(jnp.broadcast_to(mixed_low[:, None, :], (ROWS, TOPK, D)))
        outputs = lax.map(expert_apply, (buffer, w_gate, w_up, w_down))
        picked = outputs[chosen_ids, target]
        routed = lax.optimization_barrier(jnp.sum(route_weights[loop_index][:, :, None] * picked, axis=1))
        hidden = (mixed + routed).astype(jnp.bfloat16)
    return (jnp.stack(results), hidden)
```

```python
import functools

import jax
import jax.numpy as jnp
from jax import lax
from jax.experimental import pallas as pl
from jax.experimental.pallas import tpu as pltpu
from jax.sharding import PartitionSpec as P

LATENT = 512
LOOPS = 2
LANES = 128
EPSILON = 1e-06
NEG_FILL = -1e30
F32 = jnp.float32
BF16 = jnp.bfloat16
MESH = pl.DeviceIdType.MESH


def iota(shape, axis):
    return lax.broadcasted_iota(jnp.int32, shape, axis)


def wait_bytes(ref, sem):
    pltpu.make_async_copy(ref, ref, sem).wait()


def kernel(
    sizes,
    hid_in, emb_in, gains_in, q_in, cache_in, lengths, ids, route_w, wg_in, wu_in, wd_in,
    att_out, hid_out,
    hid_raw, emb_raw, gains, queries, cache, w_gu, w_down,
    hidden, emb_norm, mixed, spread, gather_t, combine_t, order, disorder,
    tiles, disp, disp_got, rows_all,
    part, sib, red, red_got, stacked, back, back_got, comb,
    att_send, att_got, lse_send, lse_got,
    load_sem, disp_s, disp_r, ag_s, ag_r, fw_s, fw_r, sib_s, sib_r, rs_s, rs_r,
    back_s, back_r, comb_s, comb_r, att_s, att_r,
):
    ne, nx, rows, jb, topk, scale = sizes
    ni = ne // 2
    nn = ni * 16
    half = 2 * ni
    fx = jb * LANES
    group = 2 * nx
    me = lax.axis_index("expert")
    cx = lax.axis_index("context")
    cp = lax.axis_index("pipe")
    my_g = cx * 2 + cp

    def device_of(g):
        return (me, lax.div(g, 2), lax.rem(g, 2))

    def x_peer(k):
        return lax.rem(cx + k, nx)

    sibling = (me, cx, 1 - cp)

    pairs = [
        (hid_in, hid_raw),
        (emb_in, emb_raw),
        (gains_in, gains),
        (q_in, queries),
        (cache_in, cache),
        (wg_in, w_gu.at[:, 0:LANES]),
        (wu_in, w_gu.at[:, LANES : 2 * LANES]),
        (wd_in, w_down),
    ]
    loads = [pltpu.make_async_copy(a, b, load_sem.at[n]) for n, (a, b) in enumerate(pairs)]
    for copy in loads:
        copy.start()

    barrier = pltpu.get_barrier_semaphore()

    def greet(i, carry):
        d = 2 * i + cp

        @pl.when(d != 0)
        def _():
            pl.semaphore_signal(
                barrier, inc=1, device_id=(lax.rem(me + d, ne), cx, cp), device_id_type=MESH
            )

        return carry

    lax.fori_loop(0, ni, greet, 0)
    for k in range(1, group):
        pl.semaphore_signal(
            barrier, inc=1, device_id=device_of(lax.rem(my_g + k, group)), device_id_type=MESH
        )

    lane = iota((8, nn), 1)
    sub = iota((8, nn), 0)
    named = (me + 2 * lax.shift_right_logical(lane, 4) + cp) & (ne - 1)
    slot = (lax.shift_right_logical(lane, 3) & 1).astype(F32)
    block = lane & 7

    def route_tables(t):
        count = jnp.zeros((8, nn), F32)
        picked = jnp.zeros((8, nn), F32)
        weight = jnp.zeros((8, nn), F32)
        for r in range(rows):
            chosen = jnp.zeros((8, nn), F32)
            value = jnp.zeros((8, nn), F32)
            for k in range(topk):
                hit = named == ids[t, r, k]
                chosen = jnp.where(hit, 1.0, chosen)
                value = jnp.where(hit, route_w[t, r, k], value)
            here = jnp.logical_and(sub == r, count == slot)
            picked = jnp.where(here, chosen, picked)
            weight = jnp.where(here, value, weight)
            count = count + chosen
        high = weight.astype(BF16).astype(F32)
        low = weight - high
        zeros = jnp.zeros((LANES - 8 * jb, nn), F32)
        wide = jnp.concatenate(
            [jnp.where(block == j, picked, 0.0) for j in range(jb)] + [zeros], axis=0
        )
        gather_t[t] = jnp.transpose(wide).astype(BF16)
        pad = jnp.zeros((64 - 8 * jb, nn), F32)
        both = []
        for piece in (high, low):
            both += [jnp.where(block == j, piece, 0.0) for j in range(jb)] + [pad]
        combine_t[t] = jnp.concatenate(both, axis=0).astype(BF16)

    route_tables(0)

    def normed(values, gain):
        return values * lax.rsqrt(jnp.mean(values * values, axis=-1, keepdims=True) + EPSILON) * gain

    hidden[...] = jnp.zeros_like(hidden)
    emb_norm[...] = jnp.zeros_like(emb_norm)
    spread[...] = jnp.zeros_like(spread)
    for copy in loads[:3]:
        copy.wait()
    hidden[0:rows, :] = hid_raw[...].astype(F32)
    for t in range(LOOPS):
        emb_norm[t, 0:rows, :] = emb_raw[t].astype(F32)
    for t in range(LOOPS):
        emb_norm[t] = normed(emb_norm[t], gains[1:2, :])

    def dispatch_tiles(t):
        mixed[...] = normed(hidden[...], gains[0:1, :]) + emb_norm[t]
        for j in range(jb):
            at = pl.multiple_of(cx * fx + j * LANES, LANES)
            spread[8 * j : 8 * j + 8, :] = mixed[:, pl.ds(at, LANES)]
        disp[t] = jnp.dot(
            gather_t[t], spread[...].astype(BF16), preferred_element_type=F32
        ).astype(BF16)

    def exchange(t, src, dst, send_sem, recv_sem, sign):
        def send(i, carry):
            d = 2 * i + cp
            at = pl.ds(pl.multiple_of(i * 16, 16), 16)

            @pl.when(d != 0)
            def _():
                pltpu.make_async_remote_copy(
                    src_ref=src.at[t, at, :],
                    dst_ref=dst.at[t, at, :],
                    send_sem=send_sem.at[t],
                    recv_sem=recv_sem.at[t],
                    device_id=(lax.rem(me + sign * d + ne, ne), cx, cp),
                    device_id_type=MESH,
                ).start()

            @pl.when(d == 0)
            def _():
                pltpu.make_async_copy(src.at[t, at, :], dst.at[t, at, :], recv_sem.at[t]).start()

            return carry

        lax.fori_loop(0, ni, send, 0)

    def exchange_sent(t, src, send_sem):
        wait_bytes(src.at[t, 16:nn, :], send_sem.at[t])

        @pl.when(cp == 1)
        def _():
            wait_bytes(src.at[t, 0:16, :], send_sem.at[t])

    def reorder_tables():
        m = iota((jb * half, nn), 0)
        n = iota((jb * half, nn), 1)
        s_i = lax.rem(m, half)
        want = lax.rem(s_i, ni) * 16 + lax.div(s_i, ni) * 8 + lax.div(m, half)
        order[...] = jnp.where(n == want, 1.0, 0.0).astype(BF16)
        n = iota((nn, jb * half), 0)
        m = iota((nn, jb * half), 1)
        s_i = lax.rem(m, half)
        want = lax.rem(s_i, ni) * 16 + lax.div(s_i, ni) * 8 + lax.div(m, half)
        disorder[...] = jnp.where(n == want, 1.0, 0.0).astype(BF16)

    def attention_partials():
        heads = queries.shape[2]
        position = my_g * LANES + iota((2 * heads, LANES), 1)
        column = iota((2 * heads, LANES), 1)
        lse_all = jnp.zeros((2 * heads, LANES), F32)
        for r in range(rows):
            q = jnp.concatenate([queries[0, r], queries[1, r]], axis=0)
            keys = cache[r]
            scores = lax.dot_general(
                q, keys, (((1,), (1,)), ((), ())), preferred_element_type=F32
            ) * scale
            live = position < lengths[r]
            scores = jnp.where(live, scores, NEG_FILL)
            top = jnp.max(scores, axis=-1, keepdims=True)
            weights = jnp.where(live, jnp.exp(scores - top), 0.0).astype(BF16)
            total = jnp.sum(weights.astype(F32), axis=-1, keepdims=True)
            summed = jnp.dot(weights, keys[:, :LATENT], preferred_element_type=F32)
            some = total > 0.0
            safe = jnp.where(some, total, 1.0)
            mean = summed / safe
            lse = jnp.where(some, top + jnp.log(safe), NEG_FILL)
            lse_all = jnp.where(column == r, lse, lse_all)
            for g in range(group):
                att_send[g, 16 * r : 16 * r + 16, :] = jnp.concatenate(
                    [mean[8 * g : 8 * g + 8], mean[heads + 8 * g : heads + 8 * g + 8]], axis=0
                ).astype(BF16)
        for g in range(group):
            lse_send[g] = jnp.concatenate(
                [lse_all[8 * g : 8 * g + 8], lse_all[heads + 8 * g : heads + 8 * g + 8]], axis=0
            )

    def attention_copies(k):
        to = lax.rem(my_g + k, group)
        return [
            pltpu.make_async_remote_copy(
                src_ref=a.at[to],
                dst_ref=b.at[k - 1],
                send_sem=att_s.at[n, k - 1],
                recv_sem=att_r.at[n, k - 1],
                device_id=device_of(to),
                device_id_type=MESH,
            )
            for n, (a, b) in enumerate(((att_send, att_got), (lse_send, lse_got)))
        ]

    def attention_send(ks):
        for k in ks:
            for copy in attention_copies(k):
                copy.start()

    def attention_finish():
        for k in range(1, group):
            for copy in attention_copies(k):
                copy.wait()
        for r in range(rows):
            tops = [lse_send[my_g][:, r : r + 1]]
            tops += [lse_got[k][:, r : r + 1] for k in range(group - 1)]
            best = functools.reduce(jnp.maximum, tops)
            factors = [jnp.exp(top - best) for top in tops]
            share = 1.0 / functools.reduce(jnp.add, factors)
            at = slice(16 * r, 16 * r + 16)
            total = att_send[my_g, at, :].astype(F32) * (factors[0] * share)
            for k in range(group - 1):
                total += att_got[k, at, :].astype(F32) * (factors[k + 1] * share)
            for t in range(LOOPS):
                att_out[t, r] = total[8 * t : 8 * t + 8].astype(BF16)

    own_rows = pl.ds(pl.multiple_of(cp * half, half), half)
    other_rows = pl.ds(pl.multiple_of((1 - cp) * half, half), half)

    def gather_copy(t, k):
        at = rows_all.at[t, cx, own_rows, :]
        if k == 0:
            return pltpu.make_async_remote_copy(
                src_ref=at, dst_ref=at, send_sem=fw_s.at[t, 0], recv_sem=fw_r.at[t, 0],
                device_id=sibling, device_id_type=MESH,
            )
        return pltpu.make_async_remote_copy(
            src_ref=at, dst_ref=at, send_sem=ag_s.at[t, k - 1], recv_sem=ag_r.at[t, k - 1],
            device_id=(me, x_peer(k), cp), device_id_type=MESH,
        )

    def forward_copy(t, k):
        at = rows_all.at[t, x_peer(nx - k), own_rows, :]
        return pltpu.make_async_remote_copy(
            src_ref=at, dst_ref=at, send_sem=fw_s.at[t, k], recv_sem=fw_r.at[t, k],
            device_id=sibling, device_id_type=MESH,
        )

    def sibling_copy(t, k):
        return pltpu.make_async_remote_copy(
            src_ref=part.at[t, k, other_rows, :], dst_ref=sib.at[t, k],
            send_sem=sib_s.at[t, k], recv_sem=sib_r.at[t, k],
            device_id=sibling, device_id_type=MESH,
        )

    def reduce_copy(t, k):
        return pltpu.make_async_remote_copy(
            src_ref=red.at[t, k - 1], dst_ref=red_got.at[t, k - 1],
            send_sem=rs_s.at[t, k - 1], recv_sem=rs_r.at[t, k - 1],
            device_id=(me, x_peer(k), cp), device_id_type=MESH,
        )

    def combine_copy(t, k):
        at = comb.at[t, my_g]
        return pltpu.make_async_remote_copy(
            src_ref=at, dst_ref=at,
            send_sem=comb_s.at[t, k - 1], recv_sem=comb_r.at[t, k - 1],
            device_id=device_of(lax.rem(my_g + k, group)), device_id_type=MESH,
        )

    near_first = [k for k in range(1, nx) if k in (1, nx - 1)]
    near_first += [k for k in range(1, nx) if k not in (1, nx - 1)]
    far_first = near_first[::-1]

    dispatch_tiles(0)
    pl.semaphore_wait(barrier, ni - 1 + cp + group - 1)

    for t in range(LOOPS):
        exchange(t, disp, disp_got, disp_s, disp_r, 1)
        if t == 0:
            reorder_tables()
            for copy in loads[3:5]:
                copy.wait()
            attention_partials()
            for copy in loads[5:]:
                copy.wait()
        else:
            attention_send([k for k in range(1, group) if k % 2 == 0])
        wait_bytes(disp_got.at[t], disp_r.at[t])
        got = jnp.dot(order[...], disp_got[t], preferred_element_type=F32).astype(BF16)
        for j in range(jb):
            rows_all[t, cx, own_rows, j * LANES : (j + 1) * LANES] = got[half * j : half * j + half]
        for k in [0] + near_first:
            gather_copy(t, k).start()
        total = jnp.zeros((2 * half, 2 * LANES), F32)
        for k in [0] + near_first:
            if k:
                gather_copy(t, k).wait_recv()
                forward_copy(t, k).start()
        for k in [0] + near_first:
            forward_copy(t, k).wait_recv()
            at = x_peer(nx - k) if k else cx
            total += jnp.dot(
                rows_all[t, at],
                w_gu[pl.ds(pl.multiple_of(at * fx, LANES), fx), :],
                preferred_element_type=F32,
            )
        gate, up = total[:, :LANES], total[:, LANES:]
        active = (gate * (1.0 / (1.0 + jnp.exp(-gate))) * up).astype(BF16)
        for k in far_first + [0]:
            at = pl.multiple_of(x_peer(k) * fx, LANES)
            part[t, k] = jnp.dot(
                active, w_down[:, pl.ds(at, fx)], preferred_element_type=F32
            ).astype(BF16)
            sibling_copy(t, k).start()
        for k in far_first:
            sibling_copy(t, k).wait_recv()
            red[t, k - 1] = (
                part[t, k, own_rows, :].astype(F32) + sib[t, k].astype(F32)
            ).astype(BF16)
            reduce_copy(t, k).start()
        sibling_copy(t, 0).wait_recv()
        summed = part[t, 0, own_rows, :].astype(F32) + sib[t, 0].astype(F32)
        for k in near_first:
            reduce_copy(t, k).wait_recv()
            summed += red_got[t, k - 1].astype(F32)
        for j in range(jb):
            stacked[half * j : half * j + half, :] = summed[:, j * LANES : (j + 1) * LANES].astype(BF16)
        back[t] = jnp.dot(disorder[...], stacked[...], preferred_element_type=F32).astype(BF16)
        exchange(t, back, back_got, back_s, back_r, -1)
        if t == 0:
            attention_send([k for k in range(1, group) if k % 2 == 1])
            route_tables(1)
        else:
            attention_finish()
        wait_bytes(back_got.at[t], back_r.at[t])
        routed = jnp.dot(combine_t[t], back_got[t], preferred_element_type=F32)
        comb[t, my_g] = (routed[0:64] + routed[64:128]).astype(BF16)
        for k in range(1, group):
            combine_copy(t, k).start()
        for k in range(1, group):
            combine_copy(t, k).wait_recv()
        for x in range(nx):
            pair = comb[t, 2 * x].astype(F32) + comb[t, 2 * x + 1].astype(F32)
            for j in range(jb):
                at = slice(x * fx + j * LANES, x * fx + (j + 1) * LANES)
                hidden[:, at] = (mixed[:, at] + pair[8 * j : 8 * j + 8]).astype(BF16).astype(F32)
        if t + 1 < LOOPS:
            dispatch_tiles(t + 1)
    hid_out[...] = hidden[0:rows, :].astype(BF16)

    for t in range(LOOPS):
        exchange_sent(t, disp, disp_s)
        exchange_sent(t, back, back_s)
        for k in range(nx):
            forward_copy(t, k).wait_send()
            sibling_copy(t, k).wait_send()
            if k:
                gather_copy(t, k).wait_send()
                reduce_copy(t, k).wait_send()
        for k in range(1, group):
            combine_copy(t, k).wait_send()


def body(
    ne, nx,
    hidden_in, draft_embeds, norm_gains, queries, latent_cache, lengths, route_ids, route_weights,
    w_gate, w_up, w_down,
):
    rows, width = hidden_in.shape
    topk = route_ids.shape[2]
    fx = width // nx
    jb = fx // LANES
    ni = ne // 2
    nn = 16 * ni
    half = 2 * ni
    group = 2 * nx
    sizes = (ne, nx, rows, jb, topk, float(queries.shape[3]) ** (-0.5))
    any_spec = pl.BlockSpec(memory_space=pl.ANY)
    smem = pl.BlockSpec(memory_space=pltpu.SMEM)
    vmem = pl.BlockSpec(memory_space=pltpu.VMEM)
    dma = pltpu.SemaphoreType.DMA
    scratch = [
        pltpu.VMEM(hidden_in.shape, BF16),
        pltpu.VMEM(draft_embeds.shape, BF16),
        pltpu.VMEM(norm_gains.shape, F32),
        pltpu.VMEM(queries.shape, BF16),
        pltpu.VMEM(latent_cache.shape, BF16),
        pltpu.VMEM((width, 2 * LANES), BF16),
        pltpu.VMEM(w_down.shape[1:], BF16),
        pltpu.VMEM((8, width), F32),
        pltpu.VMEM((LOOPS, 8, width), F32),
        pltpu.VMEM((8, width), F32),
        pltpu.VMEM((LANES, LANES), F32),
        pltpu.VMEM((LOOPS, nn, LANES), BF16),
        pltpu.VMEM((LOOPS, LANES, nn), BF16),
        pltpu.VMEM((jb * half, nn), BF16),
        pltpu.VMEM((nn, jb * half), BF16),
        pltpu.VMEM((8, LANES), F32),
        pltpu.VMEM((LOOPS, nn, LANES), BF16),
        pltpu.VMEM((LOOPS, nn, LANES), BF16),
        pltpu.VMEM((LOOPS, nx, 2 * half, fx), BF16),
        pltpu.VMEM((LOOPS, nx, 2 * half, fx), BF16),
        pltpu.VMEM((LOOPS, nx, half, fx), BF16),
        pltpu.VMEM((LOOPS, nx - 1, half, fx), BF16),
        pltpu.VMEM((LOOPS, nx - 1, half, fx), BF16),
        pltpu.VMEM((jb * half, LANES), BF16),
        pltpu.VMEM((LOOPS, nn, LANES), BF16),
        pltpu.VMEM((LOOPS, nn, LANES), BF16),
        pltpu.VMEM((LOOPS, group, 64, LANES), BF16),
        pltpu.VMEM((group, 16 * rows, LATENT), BF16),
        pltpu.VMEM((group - 1, 16 * rows, LATENT), BF16),
        pltpu.VMEM((group, 16, LANES), F32),
        pltpu.VMEM((group - 1, 16, LANES), F32),
        dma((8,)),
        dma((LOOPS,)), dma((LOOPS,)),
        dma((LOOPS, nx - 1)), dma((LOOPS, nx - 1)),
        dma((LOOPS, nx)), dma((LOOPS, nx)),
        dma((LOOPS, nx)), dma((LOOPS, nx)),
        dma((LOOPS, nx - 1)), dma((LOOPS, nx - 1)),
        dma((LOOPS,)), dma((LOOPS,)),
        dma((LOOPS, group - 1)), dma((LOOPS, group - 1)),
        dma((2, group - 1)), dma((2, group - 1)),
    ]
    heads_here = queries.shape[2] // group
    return tuple(
        pl.pallas_call(
            functools.partial(kernel, sizes),
            out_shape=(
                jax.ShapeDtypeStruct((LOOPS, rows, heads_here, LATENT), BF16),
                jax.ShapeDtypeStruct((rows, width), BF16),
            ),
            in_specs=[any_spec] * 5 + [smem] * 3 + [any_spec] * 3,
            out_specs=(vmem, vmem),
            scratch_shapes=scratch,
            compiler_params=pltpu.CompilerParams(
                collective_id=0, has_side_effects=True, vmem_limit_bytes=40 * 1024 * 1024
            ),
            name="draft_steps",
        )(
            hidden_in, draft_embeds, norm_gains, queries, latent_cache, lengths, route_ids,
            route_weights, w_gate[0], w_up[0], w_down[0],
        )
    )


def solution(mesh):
    in_specs = (
        P("expert", None),
        P(None, "expert", None),
        P(),
        P(None, "expert", None, None),
        P("expert", ("context", "pipe"), None),
        P("expert"),
        P(None, "expert", None),
        P(None, "expert", None),
        P("expert", None, ("context", "pipe")),
        P("expert", None, ("context", "pipe")),
        P("expert", ("context", "pipe"), None),
    )
    out_specs = (P(None, "expert", ("context", "pipe"), None), P("expert", None))
    run = functools.partial(body, mesh.shape["expert"], mesh.shape["context"])
    return jax.shard_map(run, mesh=mesh, in_specs=in_specs, out_specs=out_specs, check_vma=False)
```

```python
import functools

import jax
import jax.numpy as jnp
from jax import lax
from jax.experimental import pallas as pl
from jax.experimental.pallas import tpu as pltpu
from jax.sharding import PartitionSpec as P

LATENT = 512
LOOPS = 2
LANES = 128
EPSILON = 1e-06
NEG_FILL = -1e30
CHUNKS = (16, 16)
PLAN = ("A0", "A1", "C0", "C1", "E0", "E1")
F32 = jnp.float32
BF16 = jnp.bfloat16
MESH = pl.DeviceIdType.MESH


def iota(shape, axis):
    return lax.broadcasted_iota(jnp.int32, shape, axis)


def tile_offset(n, ni):
    step = lax.shift_right_logical(n + 1, 1)
    return jnp.where((n & 1) == 0, step, ni - step)


def wait_bytes(ref, sem):
    pltpu.make_async_copy(ref, ref, sem).wait()


def kernel(
    sizes,
    hid_in, emb_in, gains_in, q_in, cache_in, lengths_in, ids_in, route_w_in, wg_in, wu_in, wd_in,
    att_out, hid_out,
    lengths, ids, route_w, hid_raw, emb_raw, gains, queries, cache, w_gu, w_down,
    hidden, emb_norm, mixed, spread, gather_t, combine_t, order, disorder,
    disp, disp_got, rows_all,
    part, red_got, stacked, back, back_got, comb,
    att_send, att_got, lse_send, lse_got,
    scalar_sem, load_sem, w_s, w_r, disp_s, disp_r, ag_s, ag_r, rs_s, rs_r,
    back_s, back_r, comb_s, comb_r, att_s, att_r,
):
    ne, nx, rows, jb, topk, scale = sizes
    ni = ne // 2
    nn = ni * 16
    first = [sum(CHUNKS[:c]) for c in range(len(CHUNKS) + 1)]
    spans = [slice(16 * a, 16 * b) for a, b in zip(first, first[1:])]
    halves = [2 * n for n in CHUNKS]
    fx = jb * LANES
    group = 2 * nx
    me = lax.axis_index("expert")
    cx = lax.axis_index("context")
    cp = lax.axis_index("pipe")
    my_g = cx * 2 + cp

    def device_of(g):
        return (me, lax.div(g, 2), lax.rem(g, 2))

    def x_peer(k):
        return lax.rem(cx + k, nx)

    sibling = (me, cx, 1 - cp)

    barrier = pltpu.get_barrier_semaphore()

    def greet(n, carry):
        d = 2 * tile_offset(ni - 1 - n, ni) + cp

        @pl.when(d != 0)
        def _():
            pl.semaphore_signal(
                barrier, inc=1, device_id=(lax.rem(me + d, ne), cx, cp), device_id_type=MESH
            )

        return carry

    lax.fori_loop(0, ni, greet, 0)
    for k in range(1, group):
        pl.semaphore_signal(
            barrier, inc=1, device_id=device_of(lax.rem(my_g + k, group)), device_id_type=MESH
        )

    scalars = [
        pltpu.make_async_copy(a, b, scalar_sem.at[n])
        for n, (a, b) in enumerate(((ids_in, ids), (route_w_in, route_w), (lengths_in, lengths)))
    ]
    for copy in scalars:
        copy.start()
    pairs = [
        (hid_in, hid_raw),
        (emb_in, emb_raw),
        (gains_in, gains),
        (q_in, queries),
        (cache_in, cache),
        (wg_in, w_gu.at[:, 0:LANES]),
        (wu_in, w_gu.at[:, LANES : 2 * LANES]),
        (wd_in, w_down.at[0:LANES, :]),
    ]
    loads = [pltpu.make_async_copy(a, b, load_sem.at[n]) for n, (a, b) in enumerate(pairs)]
    for copy in loads:
        copy.start()

    lane = iota((8, nn), 1)
    sub = iota((8, nn), 0)
    named = (me + 2 * tile_offset(lax.shift_right_logical(lane, 4), ni) + cp) & (ne - 1)
    slot = (lax.shift_right_logical(lane, 3) & 1).astype(F32)
    block = lane & 7

    def route_tables(t):
        count = jnp.zeros((8, nn), F32)
        picked = jnp.zeros((8, nn), F32)
        weight = jnp.zeros((8, nn), F32)
        for r in range(rows):
            chosen = jnp.zeros((8, nn), F32)
            value = jnp.zeros((8, nn), F32)
            for k in range(topk):
                hit = named == ids[r, t, k]
                chosen = jnp.where(hit, 1.0, chosen)
                value = jnp.where(hit, route_w[r, t, k], value)
            here = jnp.logical_and(sub == r, count == slot)
            picked = jnp.where(here, chosen, picked)
            weight = jnp.where(here, value, weight)
            count = count + chosen
        high = weight.astype(BF16).astype(F32)
        low = weight - high
        zeros = jnp.zeros((LANES - 8 * jb, nn), F32)
        wide = jnp.concatenate(
            [jnp.where(block == j, picked, 0.0) for j in range(jb)] + [zeros], axis=0
        )
        gather_t[t] = jnp.transpose(wide).astype(BF16)
        pad = jnp.zeros((64 - 8 * jb, nn), F32)
        both = []
        for piece in (high, low):
            both += [jnp.where(block == j, piece, 0.0) for j in range(jb)] + [pad]
        combine_t[t] = jnp.concatenate(both, axis=0).astype(BF16)

    for copy in scalars:
        copy.wait()
    route_tables(0)

    def normed(values, gain):
        return values * lax.rsqrt(jnp.mean(values * values, axis=-1, keepdims=True) + EPSILON) * gain

    hidden[...] = jnp.zeros_like(hidden)
    emb_norm[...] = jnp.zeros_like(emb_norm)
    spread[...] = jnp.zeros_like(spread)
    for copy in loads[:3]:
        copy.wait()
    hidden[0:rows, :] = hid_raw[...].astype(F32)
    for t in range(LOOPS):
        emb_norm[t, 0:rows, :] = emb_raw[:, t, :].astype(F32)
    for t in range(LOOPS):
        emb_norm[t] = normed(emb_norm[t], gains[1:2, :])

    def dispatch_tiles(t):
        mixed[...] = normed(hidden[...], gains[0:1, :]) + emb_norm[t]
        for j in range(jb):
            at = pl.multiple_of(cx * fx + j * LANES, LANES)
            spread[8 * j : 8 * j + 8, :] = mixed[:, pl.ds(at, LANES)]
        disp[t] = jnp.dot(
            gather_t[t], spread[...].astype(BF16), preferred_element_type=F32
        ).astype(BF16)

    def chunk_of(n):
        return sum(jnp.where(n >= at, 1, 0) for at in first[1:-1])

    def exchange(t, last, count, src, dst, send_sem, recv_sem, sign):
        def send(m, carry):
            n = last - m
            d = 2 * tile_offset(n, ni) + cp
            at = pl.ds(pl.multiple_of(n * 16, 16), 16)
            done = recv_sem.at[t, chunk_of(n)]

            @pl.when(d != 0)
            def _():
                pltpu.make_async_remote_copy(
                    src_ref=src.at[t, at, :],
                    dst_ref=dst.at[t, at, :],
                    send_sem=send_sem.at[t],
                    recv_sem=done,
                    device_id=(lax.rem(me + sign * d + ne, ne), cx, cp),
                    device_id_type=MESH,
                ).start()

            @pl.when(d == 0)
            def _():
                pltpu.make_async_copy(src.at[t, at, :], dst.at[t, at, :], done).start()

            return carry

        lax.fori_loop(0, count, send, 0)

    def exchange_sent(t, src, send_sem):
        wait_bytes(src.at[t, 16:nn, :], send_sem.at[t])

        @pl.when(cp == 1)
        def _():
            wait_bytes(src.at[t, 0:16, :], send_sem.at[t])

    def reorder_tables():
        for c, (count, half) in enumerate(zip(CHUNKS, halves)):

            def place(m):
                s_i = lax.rem(m, half)
                return lax.rem(s_i, count) * 16 + lax.div(s_i, count) * 8 + lax.div(m, half)

            shape = (jb * half, 16 * count)
            order[c, : shape[0], : shape[1]] = jnp.where(
                iota(shape, 1) == place(iota(shape, 0)), 1.0, 0.0
            ).astype(BF16)
            shape = (16 * count, jb * half)
            disorder[c, : shape[0], : shape[1]] = jnp.where(
                iota(shape, 0) == place(iota(shape, 1)), 1.0, 0.0
            ).astype(BF16)

    def attention_partials():
        heads = queries.shape[2]
        position = my_g * LANES + iota((2 * heads, LANES), 1)
        column = iota((2 * heads, LANES), 1)
        lse_all = jnp.zeros((2 * heads, LANES), F32)
        for r in range(rows):
            q = jnp.concatenate([queries[0, r], queries[1, r]], axis=0)
            keys = cache[r]
            scores = lax.dot_general(
                q, keys, (((1,), (0,)), ((), ())), preferred_element_type=F32
            ) * scale
            live = position < lengths[r]
            scores = jnp.where(live, scores, NEG_FILL)
            top = jnp.max(scores, axis=-1, keepdims=True)
            weights = jnp.where(live, jnp.exp(scores - top), 0.0).astype(BF16)
            total = jnp.sum(weights.astype(F32), axis=-1, keepdims=True)
            summed = lax.dot_general(
                weights, keys[:LATENT], (((1,), (1,)), ((), ())), preferred_element_type=F32
            )
            some = total > 0.0
            safe = jnp.where(some, total, 1.0)
            mean = summed / safe
            lse = jnp.where(some, top + jnp.log(safe), NEG_FILL)
            lse_all = jnp.where(column == r, lse, lse_all)
            for g in range(group):
                att_send[g, 16 * r : 16 * r + 16, :] = jnp.concatenate(
                    [mean[8 * g : 8 * g + 8], mean[heads + 8 * g : heads + 8 * g + 8]], axis=0
                ).astype(BF16)
        for g in range(group):
            lse_send[g] = jnp.concatenate(
                [lse_all[8 * g : 8 * g + 8], lse_all[heads + 8 * g : heads + 8 * g + 8]], axis=0
            )

    def attention_copies(k):
        to = lax.rem(my_g + k, group)
        return [
            pltpu.make_async_remote_copy(
                src_ref=a.at[to],
                dst_ref=b.at[k - 1],
                send_sem=att_s.at[n, k - 1],
                recv_sem=att_r.at[n, k - 1],
                device_id=device_of(to),
                device_id_type=MESH,
            )
            for n, (a, b) in enumerate(((att_send, att_got), (lse_send, lse_got)))
        ]

    def attention_send(ks):
        for k in ks:
            for copy in attention_copies(k):
                copy.start()

    def attention_finish():
        for k in range(1, group):
            for copy in attention_copies(k):
                copy.wait()
        for r in range(rows):
            tops = [lse_send[my_g][:, r : r + 1]]
            tops += [lse_got[k][:, r : r + 1] for k in range(group - 1)]
            best = functools.reduce(jnp.maximum, tops)
            factors = [jnp.exp(top - best) for top in tops]
            share = 1.0 / functools.reduce(jnp.add, factors)
            at = slice(16 * r, 16 * r + 16)
            total = att_send[my_g, at, :].astype(F32) * (factors[0] * share)
            for k in range(group - 1):
                total += att_got[k, at, :].astype(F32) * (factors[k + 1] * share)
            for t in range(LOOPS):
                att_out[t, r] = total[8 * t : 8 * t + 8].astype(BF16)


    def gather_copy(t, c, k):
        at = rows_all.at[t, c, cx, 0 : halves[c], :]
        return pltpu.make_async_remote_copy(
            src_ref=at, dst_ref=at, send_sem=ag_s.at[t, c, k - 1], recv_sem=ag_r.at[t, c, k - 1],
            device_id=(me, x_peer(k), cp), device_id_type=MESH,
        )

    def reduce_copy(t, c, k):
        return pltpu.make_async_remote_copy(
            src_ref=part.at[t, c, k, 0 : halves[c], :],
            dst_ref=red_got.at[t, c, k - 1, 0 : halves[c], :],
            send_sem=rs_s.at[t, c, k - 1], recv_sem=rs_r.at[t, c, k - 1],
            device_id=(me, x_peer(k), cp), device_id_type=MESH,
        )

    def weight_copies():
        places = (
            (w_gu.at[:, 0 : 2 * LANES], w_gu.at[:, 2 * LANES : 4 * LANES]),
            (w_down.at[0:LANES, :], w_down.at[LANES : 2 * LANES, :]),
        )
        return [
            pltpu.make_async_remote_copy(
                src_ref=a, dst_ref=b, send_sem=w_s.at[n], recv_sem=w_r.at[n],
                device_id=sibling, device_id_type=MESH,
            )
            for n, (a, b) in enumerate(places)
        ]

    def combine_copy(t, k):
        at = comb.at[t, my_g]
        return pltpu.make_async_remote_copy(
            src_ref=at, dst_ref=at,
            send_sem=comb_s.at[t, k - 1], recv_sem=comb_r.at[t, k - 1],
            device_id=(me, x_peer(k // 2), 1 - cp if k % 2 else cp), device_id_type=MESH,
        )

    near_first = [k for k in range(1, nx) if k in (1, nx - 1)]
    near_first += [k for k in range(1, nx) if k not in (1, nx - 1)]
    far_first = near_first[::-1]
    others = [n for k in far_first for n in (2 * k, 2 * k + 1)] + [1]

    def stage_a(t, c):
        at, half = spans[c], halves[c]
        wait_bytes(disp_got.at[t, at, :], disp_r.at[t, c])
        got = jnp.dot(
            order[c, : jb * half, : 8 * half], disp_got[t, at, :], preferred_element_type=F32
        ).astype(BF16)
        for j in range(jb):
            rows_all[t, c, cx, 0:half, j * LANES : (j + 1) * LANES] = got[half * j : half * j + half]
        for k in far_first:
            gather_copy(t, c, k).start()

    def stage_c(t, c):
        half = halves[c]
        total = jnp.zeros((half, 4 * LANES), F32)
        for k in [0] + near_first:
            if k:
                gather_copy(t, c, k).wait_recv()
            at = x_peer(nx - k) if k else cx
            total += jnp.dot(
                rows_all[t, c, at, :half, :],
                w_gu[pl.ds(pl.multiple_of(at * fx, LANES), fx), :],
                preferred_element_type=F32,
            )
        gate = jnp.concatenate([total[:, :LANES], total[:, 2 * LANES : 3 * LANES]], axis=1)
        up = jnp.concatenate([total[:, LANES : 2 * LANES], total[:, 3 * LANES :]], axis=1)
        active = (gate * (1.0 / (1.0 + jnp.exp(-gate))) * up).astype(BF16)
        for k in far_first + [0]:
            at = pl.multiple_of(x_peer(k) * fx, LANES)
            part[t, c, k, :half, :] = jnp.dot(
                active, w_down[:, pl.ds(at, fx)], preferred_element_type=F32
            ).astype(BF16)
            if k:
                reduce_copy(t, c, k).start()

    def stage_e(t, c):
        half = halves[c]
        summed = part[t, c, 0, :half, :].astype(F32)
        for k in near_first:
            reduce_copy(t, c, k).wait_recv()
            summed += red_got[t, c, k - 1, :half, :].astype(F32)
        for j in range(jb):
            stacked[half * j : half * j + half, :] = summed[:, j * LANES : (j + 1) * LANES].astype(BF16)
        back[t, spans[c], :] = jnp.dot(
            disorder[c, : 8 * half, : jb * half], stacked[: jb * half, :], preferred_element_type=F32
        ).astype(BF16)
        exchange(t, first[c + 1] - 1, CHUNKS[c], back, back_got, back_s, back_r, -1)

    stages = {"A": stage_a, "C": stage_c, "E": stage_e}

    dispatch_tiles(0)
    reorder_tables()
    for copy in loads[3:5]:
        copy.wait()
    attention_partials()
    for copy in loads[5:]:
        copy.wait()
    pl.semaphore_wait(barrier, ni - 1 + cp + group - 1)

    for t in range(LOOPS):
        exchange(t, ni - 1, ni, disp, disp_got, disp_s, disp_r, 1)
        attention_send([2, 4, 6] if t == 0 else [1, 7])
        if t == 0:
            for copy in weight_copies():
                copy.start()
            for copy in weight_copies():
                copy.wait_recv()
        for step in PLAN:
            stages[step[0]](t, int(step[1:]))
        if t == 0:
            attention_send([3, 5])
            route_tables(1)
        else:
            attention_finish()
        for c, at in enumerate(spans):
            wait_bytes(back_got.at[t, at, :], back_r.at[t, c])
        routed = jnp.dot(combine_t[t], back_got[t], preferred_element_type=F32)
        comb[t, my_g] = (routed[0:64] + routed[64:128]).astype(BF16)
        for k in others:
            combine_copy(t, k).start()
        for k in others[::-1]:
            combine_copy(t, k).wait_recv()
        for x in range(nx):
            pair = comb[t, 2 * x].astype(F32) + comb[t, 2 * x + 1].astype(F32)
            for j in range(jb):
                at = slice(x * fx + j * LANES, x * fx + (j + 1) * LANES)
                hidden[:, at] = (mixed[:, at] + pair[8 * j : 8 * j + 8]).astype(BF16).astype(F32)
        if t + 1 < LOOPS:
            dispatch_tiles(t + 1)
    hid_out[...] = hidden[0:rows, :].astype(BF16)

    for copy in weight_copies():
        copy.wait_send()
    for t in range(LOOPS):
        exchange_sent(t, disp, disp_s)
        exchange_sent(t, back, back_s)
        for c in range(len(CHUNKS)):
            for k in range(1, nx):
                gather_copy(t, c, k).wait_send()
                reduce_copy(t, c, k).wait_send()
        for k in range(1, group):
            combine_copy(t, k).wait_send()


def body(
    ne, nx,
    hidden_in, draft_embeds, norm_gains, queries, latent_cache, lengths, route_ids, route_weights,
    w_gate, w_up, w_down,
):
    rows, width = hidden_in.shape
    topk = route_ids.shape[2]
    fx = width // nx
    jb = fx // LANES
    ni = ne // 2
    nn = 16 * ni
    nc = len(CHUNKS)
    most = max(CHUNKS)
    half = 2 * most
    group = 2 * nx
    sizes = (ne, nx, rows, jb, topk, float(queries.shape[3]) ** (-0.5))
    hbm = pl.BlockSpec(memory_space=pltpu.HBM)
    vmem = pl.BlockSpec(memory_space=pltpu.VMEM)
    dma = pltpu.SemaphoreType.DMA
    scratch = [
        pltpu.SMEM(lengths.shape, jnp.int32),
        pltpu.SMEM((rows, LOOPS, topk), jnp.int32),
        pltpu.SMEM((rows, LOOPS, topk), F32),
        pltpu.VMEM(hidden_in.shape, BF16),
        pltpu.VMEM((rows, LOOPS, width), BF16),
        pltpu.VMEM(norm_gains.shape, F32),
        pltpu.VMEM(queries.shape, BF16),
        pltpu.VMEM((rows, latent_cache.shape[2], LANES), BF16),
        pltpu.VMEM((width, 4 * LANES), BF16),
        pltpu.VMEM((2 * LANES, width), BF16),
        pltpu.VMEM((8, width), F32),
        pltpu.VMEM((LOOPS, 8, width), F32),
        pltpu.VMEM((8, width), F32),
        pltpu.VMEM((LANES, LANES), F32),
        pltpu.VMEM((LOOPS, nn, LANES), BF16),
        pltpu.VMEM((LOOPS, LANES, nn), BF16),
        pltpu.VMEM((nc, jb * half, 16 * most), BF16),
        pltpu.VMEM((nc, 16 * most, jb * half), BF16),
        pltpu.VMEM((LOOPS, nn, LANES), BF16),
        pltpu.VMEM((LOOPS, nn, LANES), BF16),
        pltpu.VMEM((LOOPS, nc, nx, half, fx), BF16),
        pltpu.VMEM((LOOPS, nc, nx, half, fx), BF16),
        pltpu.VMEM((LOOPS, nc, nx - 1, half, fx), BF16),
        pltpu.VMEM((jb * half, LANES), BF16),
        pltpu.VMEM((LOOPS, nn, LANES), BF16),
        pltpu.VMEM((LOOPS, nn, LANES), BF16),
        pltpu.VMEM((LOOPS, group, 64, LANES), BF16),
        pltpu.VMEM((group, 16 * rows, LATENT), BF16),
        pltpu.VMEM((group - 1, 16 * rows, LATENT), BF16),
        pltpu.VMEM((group, 16, LANES), F32),
        pltpu.VMEM((group - 1, 16, LANES), F32),
        dma((3,)), dma((8,)), dma((2,)), dma((2,)),
        dma((LOOPS,)), dma((LOOPS, nc)),
        dma((LOOPS, nc, nx - 1)), dma((LOOPS, nc, nx - 1)),
        dma((LOOPS, nc, nx - 1)), dma((LOOPS, nc, nx - 1)),
        dma((LOOPS,)), dma((LOOPS, nc)),
        dma((LOOPS, group - 1)), dma((LOOPS, group - 1)),
        dma((2, group - 1)), dma((2, group - 1)),
    ]
    heads_here = queries.shape[2] // group
    return tuple(
        pl.pallas_call(
            functools.partial(kernel, sizes),
            out_shape=(
                jax.ShapeDtypeStruct((LOOPS, rows, heads_here, LATENT), BF16),
                jax.ShapeDtypeStruct((rows, width), BF16),
            ),
            in_specs=[hbm] * 11,
            out_specs=(vmem, vmem),
            scratch_shapes=scratch,
            compiler_params=pltpu.CompilerParams(
                collective_id=0, has_side_effects=True, vmem_limit_bytes=60 * 1024 * 1024
            ),
            name="draft_steps",
        )(
            hidden_in, jnp.swapaxes(draft_embeds, 0, 1), norm_gains, queries,
            jnp.swapaxes(latent_cache, 1, 2), lengths, jnp.swapaxes(route_ids, 0, 1),
            jnp.swapaxes(route_weights, 0, 1), w_gate[0], w_up[0], w_down[0],
        )
    )


def solution(mesh):
    in_specs = (
        P("expert", None),
        P(None, "expert", None),
        P(),
        P(None, "expert", None, None),
        P("expert", ("context", "pipe"), None),
        P("expert"),
        P(None, "expert", None),
        P(None, "expert", None),
        P("expert", None, ("context", "pipe")),
        P("expert", None, ("context", "pipe")),
        P("expert", ("context", "pipe"), None),
    )
    out_specs = (P(None, "expert", ("context", "pipe"), None), P("expert", None))
    run = functools.partial(body, mesh.shape["expert"], mesh.shape["context"])
    return jax.shard_map(run, mesh=mesh, in_specs=in_specs, out_specs=out_specs, check_vma=False)
```

```python
import functools

import jax
import jax.numpy as jnp
from jax import lax
from jax.experimental import pallas as pl
from jax.experimental.pallas import tpu as pltpu
from jax.sharding import PartitionSpec as P

LATENT = 512
LOOPS = 2
LANES = 128
EPSILON = 1e-06
NEG_FILL = -1e30
CHUNKS = (16, 16)
PLAN = ("A0", "A1", "C0", "C1", "E0", "E1")
F32 = jnp.float32
BF16 = jnp.bfloat16
MESH = pl.DeviceIdType.MESH


def iota(shape, axis):
    return lax.broadcasted_iota(jnp.int32, shape, axis)


def tile_offset(n, ni):
    step = lax.shift_right_logical(n + 1, 1)
    return jnp.where((n & 1) == 0, step, ni - step)


def wait_bytes(ref, sem):
    pltpu.make_async_copy(ref, ref, sem).wait()


def kernel(
    sizes,
    hid_in, emb_in, gains_in, q_in, cache_in, lengths_in, ids_in, route_w_in, wg_in, wu_in, wd_in,
    att_out, hid_out,
    lengths, ids, route_w, hid_raw, emb_raw, gains, queries, cache, w_gu, w_down,
    hidden, emb_norm, mixed, spread, gather_t, combine_t, order, disorder,
    disp, disp_got, rows_all,
    part, red_got, stacked, back, back_got, comb,
    att_send, att_got, lse_send, lse_got,
    scalar_sem, load_sem, w_s, w_r, disp_s, disp_r, ag_s, ag_r, rs_s, rs_r,
    back_s, back_r, comb_s, comb_r, att_s, att_r,
):
    ne, nx, rows, jb, topk, scale = sizes
    ni = ne // 2
    nn = ni * 16
    first = [sum(CHUNKS[:c]) for c in range(len(CHUNKS) + 1)]
    spans = [slice(16 * a, 16 * b) for a, b in zip(first, first[1:])]
    halves = [2 * n for n in CHUNKS]
    fx = jb * LANES
    group = 2 * nx
    me = lax.axis_index("expert")
    cx = lax.axis_index("context")
    cp = lax.axis_index("pipe")
    my_g = cx * 2 + cp

    def device_of(g):
        return (me, lax.div(g, 2), lax.rem(g, 2))

    def x_peer(k):
        return lax.rem(cx + k, nx)

    sibling = (me, cx, 1 - cp)

    barrier = pltpu.get_barrier_semaphore()

    def greet(n, carry):
        d = 2 * tile_offset(ni - 1 - n, ni) + cp

        @pl.when(d != 0)
        def _():
            pl.semaphore_signal(
                barrier, inc=1, device_id=(lax.rem(me + d, ne), cx, cp), device_id_type=MESH
            )

        return carry

    lax.fori_loop(0, ni, greet, 0)
    for k in range(1, group):
        pl.semaphore_signal(
            barrier, inc=1, device_id=device_of(lax.rem(my_g + k, group)), device_id_type=MESH
        )

    scalars = [
        pltpu.make_async_copy(a, b, scalar_sem.at[n])
        for n, (a, b) in enumerate(((ids_in, ids), (route_w_in, route_w), (lengths_in, lengths)))
    ]
    for copy in scalars:
        copy.start()
    pairs = [
        (hid_in, hid_raw),
        (emb_in, emb_raw),
        (gains_in, gains),
        (q_in, queries),
        (cache_in, cache),
        (wg_in, w_gu.at[:, 0:LANES]),
        (wu_in, w_gu.at[:, LANES : 2 * LANES]),
        (wd_in, w_down.at[0:LANES, :]),
    ]
    loads = [pltpu.make_async_copy(a, b, load_sem.at[n]) for n, (a, b) in enumerate(pairs)]
    for copy in loads:
        copy.start()

    lane = iota((8, nn), 1)
    sub = iota((8, nn), 0)
    named = (me + 2 * tile_offset(lax.shift_right_logical(lane, 4), ni) + cp) & (ne - 1)
    slot = (lax.shift_right_logical(lane, 3) & 1).astype(F32)
    block = lane & 7

    def route_tables(t):
        count = jnp.zeros((8, nn), F32)
        picked = jnp.zeros((8, nn), F32)
        weight = jnp.zeros((8, nn), F32)
        for r in range(rows):
            chosen = jnp.zeros((8, nn), F32)
            value = jnp.zeros((8, nn), F32)
            for k in range(topk):
                hit = named == ids[r, t, k]
                chosen = jnp.where(hit, 1.0, chosen)
                value = jnp.where(hit, route_w[r, t, k], value)
            here = jnp.logical_and(sub == r, count == slot)
            picked = jnp.where(here, chosen, picked)
            weight = jnp.where(here, value, weight)
            count = count + chosen
        high = weight.astype(BF16).astype(F32)
        low = weight - high
        zeros = jnp.zeros((LANES - 8 * jb, nn), F32)
        wide = jnp.concatenate(
            [jnp.where(block == j, picked, 0.0) for j in range(jb)] + [zeros], axis=0
        )
        gather_t[t] = jnp.transpose(wide).astype(BF16)
        pad = jnp.zeros((64 - 8 * jb, nn), F32)
        both = []
        for piece in (high, low):
            both += [jnp.where(block == j, piece, 0.0) for j in range(jb)] + [pad]
        combine_t[t] = jnp.concatenate(both, axis=0).astype(BF16)

    for copy in scalars:
        copy.wait()
    route_tables(0)

    def normed(values, gain):
        return values * lax.rsqrt(jnp.mean(values * values, axis=-1, keepdims=True) + EPSILON) * gain

    hidden[...] = jnp.zeros_like(hidden)
    emb_norm[...] = jnp.zeros_like(emb_norm)
    spread[...] = jnp.zeros_like(spread)
    for copy in loads[:3]:
        copy.wait()
    hidden[0:rows, :] = hid_raw[...].astype(F32)
    for t in range(LOOPS):
        emb_norm[t, 0:rows, :] = emb_raw[:, t, :].astype(F32)
    for t in range(LOOPS):
        emb_norm[t] = normed(emb_norm[t], gains[1:2, :])

    def dispatch_tiles(t):
        mixed[...] = normed(hidden[...], gains[0:1, :]) + emb_norm[t]
        for j in range(jb):
            at = pl.multiple_of(cx * fx + j * LANES, LANES)
            spread[8 * j : 8 * j + 8, :] = mixed[:, pl.ds(at, LANES)]
        disp[t] = jnp.dot(
            gather_t[t], spread[...].astype(BF16), preferred_element_type=F32
        ).astype(BF16)

    def chunk_of(n):
        return sum(jnp.where(n >= at, 1, 0) for at in first[1:-1])

    def exchange(t, last, count, src, dst, send_sem, recv_sem, sign):
        def send(m, carry):
            n = last - m
            d = 2 * tile_offset(n, ni) + cp
            at = pl.ds(pl.multiple_of(n * 16, 16), 16)
            done = recv_sem.at[t, chunk_of(n)]

            @pl.when(d != 0)
            def _():
                pltpu.make_async_remote_copy(
                    src_ref=src.at[t, at, :],
                    dst_ref=dst.at[t, at, :],
                    send_sem=send_sem.at[t],
                    recv_sem=done,
                    device_id=(lax.rem(me + sign * d + ne, ne), cx, cp),
                    device_id_type=MESH,
                ).start()

            @pl.when(d == 0)
            def _():
                pltpu.make_async_copy(src.at[t, at, :], dst.at[t, at, :], done).start()

            return carry

        lax.fori_loop(0, count, send, 0)

    def exchange_sent(t, src, send_sem):
        wait_bytes(src.at[t, 16:nn, :], send_sem.at[t])

        @pl.when(cp == 1)
        def _():
            wait_bytes(src.at[t, 0:16, :], send_sem.at[t])

    def reorder_tables():
        for c, (count, half) in enumerate(zip(CHUNKS, halves)):

            def place(m):
                s_i = lax.rem(m, half)
                return lax.rem(s_i, count) * 16 + lax.div(s_i, count) * 8 + lax.div(m, half)

            shape = (jb * half, 16 * count)
            order[c, : shape[0], : shape[1]] = jnp.where(
                iota(shape, 1) == place(iota(shape, 0)), 1.0, 0.0
            ).astype(BF16)
            shape = (16 * count, jb * half)
            disorder[c, : shape[0], : shape[1]] = jnp.where(
                iota(shape, 0) == place(iota(shape, 1)), 1.0, 0.0
            ).astype(BF16)

    def attention_partials():
        heads = queries.shape[2]
        position = my_g * LANES + iota((2 * heads, LANES), 1)
        column = iota((2 * heads, LANES), 1)
        lse_all = jnp.zeros((2 * heads, LANES), F32)
        for r in range(rows):
            q = jnp.concatenate([queries[0, r], queries[1, r]], axis=0)
            keys = cache[r]
            scores = lax.dot_general(
                q, keys, (((1,), (0,)), ((), ())), preferred_element_type=F32
            ) * scale
            live = position < lengths[r]
            scores = jnp.where(live, scores, NEG_FILL)
            top = jnp.max(scores, axis=-1, keepdims=True)
            weights = jnp.where(live, jnp.exp(scores - top), 0.0).astype(BF16)
            total = jnp.sum(weights.astype(F32), axis=-1, keepdims=True)
            summed = lax.dot_general(
                weights, keys[:LATENT], (((1,), (1,)), ((), ())), preferred_element_type=F32
            )
            some = total > 0.0
            safe = jnp.where(some, total, 1.0)
            mean = summed / safe
            lse = jnp.where(some, top + jnp.log(safe), NEG_FILL)
            lse_all = jnp.where(column == r, lse, lse_all)
            for g in range(group):
                att_send[g, 16 * r : 16 * r + 16, :] = jnp.concatenate(
                    [mean[8 * g : 8 * g + 8], mean[heads + 8 * g : heads + 8 * g + 8]], axis=0
                ).astype(BF16)
        for g in range(group):
            lse_send[g] = jnp.concatenate(
                [lse_all[8 * g : 8 * g + 8], lse_all[heads + 8 * g : heads + 8 * g + 8]], axis=0
            )

    def attention_copies(k):
        to = lax.rem(my_g + k, group)
        return [
            pltpu.make_async_remote_copy(
                src_ref=a.at[to],
                dst_ref=b.at[k - 1],
                send_sem=att_s.at[n, k - 1],
                recv_sem=att_r.at[n, k - 1],
                device_id=device_of(to),
                device_id_type=MESH,
            )
            for n, (a, b) in enumerate(((att_send, att_got), (lse_send, lse_got)))
        ]

    def attention_send(ks):
        for k in ks:
            for copy in attention_copies(k):
                copy.start()

    def attention_finish():
        for k in range(1, group):
            for copy in attention_copies(k):
                copy.wait()
        for r in range(rows):
            tops = [lse_send[my_g][:, r : r + 1]]
            tops += [lse_got[k][:, r : r + 1] for k in range(group - 1)]
            best = functools.reduce(jnp.maximum, tops)
            factors = [jnp.exp(top - best) for top in tops]
            share = 1.0 / functools.reduce(jnp.add, factors)
            at = slice(16 * r, 16 * r + 16)
            total = att_send[my_g, at, :].astype(F32) * (factors[0] * share)
            for k in range(group - 1):
                total += att_got[k, at, :].astype(F32) * (factors[k + 1] * share)
            for t in range(LOOPS):
                att_out[t, r] = total[8 * t : 8 * t + 8].astype(BF16)


    def gather_copy(t, c, k):
        at = rows_all.at[t, c, cx, 0 : halves[c], :]
        return pltpu.make_async_remote_copy(
            src_ref=at, dst_ref=at, send_sem=ag_s.at[t, c, k - 1], recv_sem=ag_r.at[t, c, k - 1],
            device_id=(me, x_peer(k), cp), device_id_type=MESH,
        )

    def reduce_copy(t, c, k):
        return pltpu.make_async_remote_copy(
            src_ref=part.at[t, c, k, 0 : halves[c], :],
            dst_ref=red_got.at[t, c, k - 1, 0 : halves[c], :],
            send_sem=rs_s.at[t, c, k - 1], recv_sem=rs_r.at[t, c, k - 1],
            device_id=(me, x_peer(k), cp), device_id_type=MESH,
        )

    def weight_copies():
        places = (
            (w_gu.at[:, 0 : 2 * LANES], w_gu.at[:, 2 * LANES : 4 * LANES]),
            (w_down.at[0:LANES, :], w_down.at[LANES : 2 * LANES, :]),
        )
        return [
            pltpu.make_async_remote_copy(
                src_ref=a, dst_ref=b, send_sem=w_s.at[n], recv_sem=w_r.at[n],
                device_id=sibling, device_id_type=MESH,
            )
            for n, (a, b) in enumerate(places)
        ]

    def combine_copy(t, k):
        at = comb.at[t, my_g]
        return pltpu.make_async_remote_copy(
            src_ref=at, dst_ref=at,
            send_sem=comb_s.at[t, k - 1], recv_sem=comb_r.at[t, k - 1],
            device_id=(me, x_peer(k // 2), 1 - cp if k % 2 else cp), device_id_type=MESH,
        )

    near_first = [k for k in range(1, nx) if k in (1, nx - 1)]
    near_first += [k for k in range(1, nx) if k not in (1, nx - 1)]
    far_first = near_first[::-1]
    others = [n for k in far_first for n in (2 * k, 2 * k + 1)] + [1]

    def stage_a(t, c):
        at, half = spans[c], halves[c]
        wait_bytes(disp_got.at[t, at, :], disp_r.at[t, c])
        got = jnp.dot(
            order[c, : jb * half, : 8 * half], disp_got[t, at, :], preferred_element_type=F32
        ).astype(BF16)
        for j in range(jb):
            rows_all[t, c, cx, 0:half, j * LANES : (j + 1) * LANES] = got[half * j : half * j + half]
        for k in far_first:
            gather_copy(t, c, k).start()

    def stage_c(t, c):
        half = halves[c]
        total = jnp.zeros((half, 4 * LANES), F32)
        for k in [0] + near_first:
            if k:
                gather_copy(t, c, k).wait_recv()
            at = x_peer(nx - k) if k else cx
            total += jnp.dot(
                rows_all[t, c, at, :half, :],
                w_gu[pl.ds(pl.multiple_of(at * fx, LANES), fx), :],
                preferred_element_type=F32,
            )
        gate = jnp.concatenate([total[:, :LANES], total[:, 2 * LANES : 3 * LANES]], axis=1)
        up = jnp.concatenate([total[:, LANES : 2 * LANES], total[:, 3 * LANES :]], axis=1)
        active = (gate * (1.0 / (1.0 + jnp.exp(-gate))) * up).astype(BF16)
        for k in far_first + [0]:
            at = pl.multiple_of(x_peer(k) * fx, LANES)
            part[t, c, k, :half, :] = jnp.dot(
                active, w_down[:, pl.ds(at, fx)], preferred_element_type=F32
            ).astype(BF16)
            if k:
                reduce_copy(t, c, k).start()

    def stage_e(t, c):
        half = halves[c]
        summed = part[t, c, 0, :half, :].astype(F32)
        for k in near_first:
            reduce_copy(t, c, k).wait_recv()
            summed += red_got[t, c, k - 1, :half, :].astype(F32)
        for j in range(jb):
            stacked[half * j : half * j + half, :] = summed[:, j * LANES : (j + 1) * LANES].astype(BF16)
        back[t, spans[c], :] = jnp.dot(
            disorder[c, : 8 * half, : jb * half], stacked[: jb * half, :], preferred_element_type=F32
        ).astype(BF16)
        exchange(t, first[c + 1] - 1, CHUNKS[c], back, back_got, back_s, back_r, -1)

    stages = {"A": stage_a, "C": stage_c, "E": stage_e}

    dispatch_tiles(0)
    reorder_tables()
    for copy in loads[3:5]:
        copy.wait()
    attention_partials()
    for copy in loads[5:]:
        copy.wait()
    pl.semaphore_wait(barrier, ni - 1 + cp + group - 1)

    for t in range(LOOPS):
        exchange(t, ni - 1, ni, disp, disp_got, disp_s, disp_r, 1)
        attention_send([4, 3, 5] if t == 0 else [2, 6, 7])
        if t == 0:
            for copy in weight_copies():
                copy.start()
            for copy in weight_copies():
                copy.wait_recv()
        for step in PLAN:
            stages[step[0]](t, int(step[1:]))
        if t == 0:
            attention_send([1])
            route_tables(1)
        else:
            attention_finish()
            for copy in weight_copies():
                copy.wait_send()
            exchange_sent(0, back, back_s)
            for u in range(LOOPS):
                exchange_sent(u, disp, disp_s)
                for c in range(len(CHUNKS)):
                    for k in range(1, nx):
                        gather_copy(u, c, k).wait_send()
                        reduce_copy(u, c, k).wait_send()
            for k in range(1, group):
                combine_copy(0, k).wait_send()
        routed = jnp.zeros((LANES, LANES), F32)
        for c, at in enumerate(spans):
            wait_bytes(back_got.at[t, at, :], back_r.at[t, c])
            routed += jnp.dot(combine_t[t, :, at], back_got[t, at, :], preferred_element_type=F32)
        comb[t, my_g] = (routed[0:64] + routed[64:128]).astype(BF16)
        for k in others:
            combine_copy(t, k).start()
        for k in others[::-1]:
            combine_copy(t, k).wait_recv()
        for x in range(nx):
            pair = comb[t, 2 * x].astype(F32) + comb[t, 2 * x + 1].astype(F32)
            for j in range(jb):
                at = slice(x * fx + j * LANES, x * fx + (j + 1) * LANES)
                hidden[:, at] = (mixed[:, at] + pair[8 * j : 8 * j + 8]).astype(BF16).astype(F32)
        if t + 1 < LOOPS:
            dispatch_tiles(t + 1)
    hid_out[...] = hidden[0:rows, :].astype(BF16)

    exchange_sent(1, back, back_s)
    for k in range(1, group):
        combine_copy(1, k).wait_send()


def body(
    ne, nx,
    hidden_in, draft_embeds, norm_gains, queries, latent_cache, lengths, route_ids, route_weights,
    w_gate, w_up, w_down,
):
    rows, width = hidden_in.shape
    topk = route_ids.shape[2]
    fx = width // nx
    jb = fx // LANES
    ni = ne // 2
    nn = 16 * ni
    nc = len(CHUNKS)
    most = max(CHUNKS)
    half = 2 * most
    group = 2 * nx
    sizes = (ne, nx, rows, jb, topk, float(queries.shape[3]) ** (-0.5))
    hbm = pl.BlockSpec(memory_space=pltpu.HBM)
    vmem = pl.BlockSpec(memory_space=pltpu.VMEM)
    dma = pltpu.SemaphoreType.DMA
    scratch = [
        pltpu.SMEM(lengths.shape, jnp.int32),
        pltpu.SMEM((rows, LOOPS, topk), jnp.int32),
        pltpu.SMEM((rows, LOOPS, topk), F32),
        pltpu.VMEM(hidden_in.shape, BF16),
        pltpu.VMEM((rows, LOOPS, width), BF16),
        pltpu.VMEM(norm_gains.shape, F32),
        pltpu.VMEM(queries.shape, BF16),
        pltpu.VMEM((rows, latent_cache.shape[2], LANES), BF16),
        pltpu.VMEM((width, 4 * LANES), BF16),
        pltpu.VMEM((2 * LANES, width), BF16),
        pltpu.VMEM((8, width), F32),
        pltpu.VMEM((LOOPS, 8, width), F32),
        pltpu.VMEM((8, width), F32),
        pltpu.VMEM((LANES, LANES), F32),
        pltpu.VMEM((LOOPS, nn, LANES), BF16),
        pltpu.VMEM((LOOPS, LANES, nn), BF16),
        pltpu.VMEM((nc, jb * half, 16 * most), BF16),
        pltpu.VMEM((nc, 16 * most, jb * half), BF16),
        pltpu.VMEM((LOOPS, nn, LANES), BF16),
        pltpu.VMEM((LOOPS, nn, LANES), BF16),
        pltpu.VMEM((LOOPS, nc, nx, half, fx), BF16),
        pltpu.VMEM((LOOPS, nc, nx, half, fx), BF16),
        pltpu.VMEM((LOOPS, nc, nx - 1, half, fx), BF16),
        pltpu.VMEM((jb * half, LANES), BF16),
        pltpu.VMEM((LOOPS, nn, LANES), BF16),
        pltpu.VMEM((LOOPS, nn, LANES), BF16),
        pltpu.VMEM((LOOPS, group, 64, LANES), BF16),
        pltpu.VMEM((group, 16 * rows, LATENT), BF16),
        pltpu.VMEM((group - 1, 16 * rows, LATENT), BF16),
        pltpu.VMEM((group, 16, LANES), F32),
        pltpu.VMEM((group - 1, 16, LANES), F32),
        dma((3,)), dma((8,)), dma((2,)), dma((2,)),
        dma((LOOPS,)), dma((LOOPS, nc)),
        dma((LOOPS, nc, nx - 1)), dma((LOOPS, nc, nx - 1)),
        dma((LOOPS, nc, nx - 1)), dma((LOOPS, nc, nx - 1)),
        dma((LOOPS,)), dma((LOOPS, nc)),
        dma((LOOPS, group - 1)), dma((LOOPS, group - 1)),
        dma((2, group - 1)), dma((2, group - 1)),
    ]
    heads_here = queries.shape[2] // group
    return tuple(
        pl.pallas_call(
            functools.partial(kernel, sizes),
            out_shape=(
                jax.ShapeDtypeStruct((LOOPS, rows, heads_here, LATENT), BF16),
                jax.ShapeDtypeStruct((rows, width), BF16),
            ),
            in_specs=[hbm] * 11,
            out_specs=(vmem, vmem),
            scratch_shapes=scratch,
            compiler_params=pltpu.CompilerParams(
                collective_id=0, has_side_effects=True, vmem_limit_bytes=60 * 1024 * 1024
            ),
            name="draft_steps",
        )(
            hidden_in, jnp.swapaxes(draft_embeds, 0, 1), norm_gains, queries,
            jnp.swapaxes(latent_cache, 1, 2), lengths, jnp.swapaxes(route_ids, 0, 1),
            jnp.swapaxes(route_weights, 0, 1), w_gate[0], w_up[0], w_down[0],
        )
    )


def solution(mesh):
    in_specs = (
        P("expert", None),
        P(None, "expert", None),
        P(),
        P(None, "expert", None, None),
        P("expert", ("context", "pipe"), None),
        P("expert"),
        P(None, "expert", None),
        P(None, "expert", None),
        P("expert", None, ("context", "pipe")),
        P("expert", None, ("context", "pipe")),
        P("expert", ("context", "pipe"), None),
    )
    out_specs = (P(None, "expert", ("context", "pipe"), None), P("expert", None))
    run = functools.partial(body, mesh.shape["expert"], mesh.shape["context"])
    return jax.shard_map(run, mesh=mesh, in_specs=in_specs, out_specs=out_specs, check_vma=False)
```

```python
import functools

import jax
import jax.numpy as jnp
from jax import lax
from jax.experimental import pallas as pl
from jax.experimental.pallas import tpu as pltpu
from jax.sharding import PartitionSpec as P

LATENT = 512
LOOPS = 2
LANES = 128
EPSILON = 1e-06
NEG_FILL = -1e30
CHUNKS = (16, 16)
PLAN = ("A0", "A1", "C0", "C1", "E0", "E1")
F32 = jnp.float32
BF16 = jnp.bfloat16
MESH = pl.DeviceIdType.MESH


def iota(shape, axis):
    return lax.broadcasted_iota(jnp.int32, shape, axis)


def tile_offset(n, ni):
    step = lax.shift_right_logical(n + 1, 1)
    return jnp.where((n & 1) == 0, step, ni - step)


def wait_bytes(ref, sem):
    pltpu.make_async_copy(ref, ref, sem).wait()


def kernel(
    sizes,
    hid_in, emb_in, gains_in, q_in, cache_in, lengths_in, ids_in, route_w_in, wg_in, wu_in, wd_in,
    att_out, hid_out,
    lengths, ids, route_w, hid_raw, emb_raw, gains, queries, cache, w_gu, w_down,
    hidden, emb_norm, mixed, spread, gather_t, combine_t, order, disorder,
    disp, disp_got, rows_all,
    part, red_got, stacked, back, back_got, comb,
    att_send, att_got, lse_send, lse_got,
    scalar_sem, load_sem, w_s, w_r, disp_s, disp_r, ag_s, ag_r, rs_s, rs_r,
    back_s, back_r, comb_s, comb_r, att_s, att_r,
):
    ne, nx, rows, jb, topk, scale = sizes
    ni = ne // 2
    nn = ni * 16
    first = [sum(CHUNKS[:c]) for c in range(len(CHUNKS) + 1)]
    spans = [slice(16 * a, 16 * b) for a, b in zip(first, first[1:])]
    halves = [2 * n for n in CHUNKS]
    fx = jb * LANES
    group = 2 * nx
    me = lax.axis_index("expert")
    cx = lax.axis_index("context")
    cp = lax.axis_index("pipe")
    my_g = cx * 2 + cp

    def device_of(g):
        return (me, lax.div(g, 2), lax.rem(g, 2))

    def x_peer(k):
        return lax.rem(cx + k, nx)

    sibling = (me, cx, 1 - cp)

    barrier = pltpu.get_barrier_semaphore()

    def greet(n, carry):
        d = 2 * tile_offset(ni - 1 - n, ni) + cp

        @pl.when(d != 0)
        def _():
            pl.semaphore_signal(
                barrier, inc=1, device_id=(lax.rem(me + d, ne), cx, cp), device_id_type=MESH
            )

        return carry

    lax.fori_loop(0, ni, greet, 0)
    for k in range(1, group):
        pl.semaphore_signal(
            barrier, inc=1, device_id=device_of(lax.rem(my_g + k, group)), device_id_type=MESH
        )

    scalars = [
        pltpu.make_async_copy(a, b, scalar_sem.at[n])
        for n, (a, b) in enumerate(((ids_in, ids), (route_w_in, route_w), (lengths_in, lengths)))
    ]
    for copy in scalars:
        copy.start()
    pairs = [
        (hid_in, hid_raw),
        (emb_in, emb_raw),
        (gains_in, gains),
        (q_in, queries),
        (cache_in, cache),
        (wg_in, w_gu.at[:, 0:LANES]),
        (wu_in, w_gu.at[:, LANES : 2 * LANES]),
        (wd_in, w_down.at[0:LANES, :]),
    ]
    loads = [pltpu.make_async_copy(a, b, load_sem.at[n]) for n, (a, b) in enumerate(pairs)]
    for copy in loads:
        copy.start()

    lane = iota((8, nn), 1)
    sub = iota((8, nn), 0)
    named = (me + 2 * tile_offset(lax.shift_right_logical(lane, 4), ni) + cp) & (ne - 1)
    slot = (lax.shift_right_logical(lane, 3) & 1).astype(F32)
    block = lane & 7

    def route_tables(t):
        count = jnp.zeros((8, nn), F32)
        picked = jnp.zeros((8, nn), F32)
        weight = jnp.zeros((8, nn), F32)
        for r in range(rows):
            chosen = jnp.zeros((8, nn), F32)
            value = jnp.zeros((8, nn), F32)
            for k in range(topk):
                hit = named == ids[r, t, k]
                chosen = jnp.where(hit, 1.0, chosen)
                value = jnp.where(hit, route_w[r, t, k], value)
            here = jnp.logical_and(sub == r, count == slot)
            picked = jnp.where(here, chosen, picked)
            weight = jnp.where(here, value, weight)
            count = count + chosen
        high = weight.astype(BF16).astype(F32)
        low = weight - high
        zeros = jnp.zeros((LANES - 8 * jb, nn), F32)
        wide = jnp.concatenate(
            [jnp.where(block == j, picked, 0.0) for j in range(jb)] + [zeros], axis=0
        )
        gather_t[t] = jnp.transpose(wide).astype(BF16)
        pad = jnp.zeros((64 - 8 * jb, nn), F32)
        both = []
        for piece in (high, low):
            both += [jnp.where(block == j, piece, 0.0) for j in range(jb)] + [pad]
        combine_t[t] = jnp.concatenate(both, axis=0).astype(BF16)

    for copy in scalars:
        copy.wait()
    route_tables(0)

    def normed(values, gain):
        return values * lax.rsqrt(jnp.mean(values * values, axis=-1, keepdims=True) + EPSILON) * gain

    hidden[...] = jnp.zeros_like(hidden)
    emb_norm[...] = jnp.zeros_like(emb_norm)
    spread[...] = jnp.zeros_like(spread)
    for copy in loads[:3]:
        copy.wait()
    hidden[0:rows, :] = hid_raw[...].astype(F32)
    for t in range(LOOPS):
        emb_norm[t, 0:rows, :] = emb_raw[:, t, :].astype(F32)
    for t in range(LOOPS):
        emb_norm[t] = normed(emb_norm[t], gains[1:2, :])

    def dispatch_tiles(t):
        mixed[...] = normed(hidden[...], gains[0:1, :]) + emb_norm[t]
        for j in range(jb):
            at = pl.multiple_of(cx * fx + j * LANES, LANES)
            spread[8 * j : 8 * j + 8, :] = mixed[:, pl.ds(at, LANES)]
        disp[t] = jnp.dot(
            gather_t[t], spread[...].astype(BF16), preferred_element_type=F32
        ).astype(BF16)

    def chunk_of(n):
        return sum(jnp.where(n >= at, 1, 0) for at in first[1:-1])

    def exchange(t, last, count, src, dst, send_sem, recv_sem, sign):
        def send(m, carry):
            n = last - m
            d = 2 * tile_offset(n, ni) + cp
            at = pl.ds(pl.multiple_of(n * 16, 16), 16)
            done = recv_sem.at[t, chunk_of(n)]

            @pl.when(d != 0)
            def _():
                pltpu.make_async_remote_copy(
                    src_ref=src.at[t, at, :],
                    dst_ref=dst.at[t, at, :],
                    send_sem=send_sem.at[t],
                    recv_sem=done,
                    device_id=(lax.rem(me + sign * d + ne, ne), cx, cp),
                    device_id_type=MESH,
                ).start()

            @pl.when(d == 0)
            def _():
                pltpu.make_async_copy(src.at[t, at, :], dst.at[t, at, :], done).start()

            return carry

        lax.fori_loop(0, count, send, 0)

    def exchange_sent(t, src, send_sem):
        wait_bytes(src.at[t, 16:nn, :], send_sem.at[t])

        @pl.when(cp == 1)
        def _():
            wait_bytes(src.at[t, 0:16, :], send_sem.at[t])

    def reorder_tables():
        for c, (count, half) in enumerate(zip(CHUNKS, halves)):

            def place(m):
                s_i = lax.rem(m, half)
                return lax.rem(s_i, count) * 16 + lax.div(s_i, count) * 8 + lax.div(m, half)

            shape = (jb * half, 16 * count)
            order[c, : shape[0], : shape[1]] = jnp.where(
                iota(shape, 1) == place(iota(shape, 0)), 1.0, 0.0
            ).astype(BF16)
            shape = (16 * count, jb * half)
            disorder[c, : shape[0], : shape[1]] = jnp.where(
                iota(shape, 0) == place(iota(shape, 1)), 1.0, 0.0
            ).astype(BF16)

    def attention_partials():
        heads = queries.shape[2]
        position = my_g * LANES + iota((2 * heads, LANES), 1)
        column = iota((2 * heads, LANES), 1)
        lse_all = jnp.zeros((2 * heads, LANES), F32)
        for r in range(rows):
            q = jnp.concatenate([queries[0, r], queries[1, r]], axis=0)
            keys = cache[r]
            scores = lax.dot_general(
                q, keys, (((1,), (0,)), ((), ())), preferred_element_type=F32
            ) * scale
            live = position < lengths[r]
            scores = jnp.where(live, scores, NEG_FILL)
            top = jnp.max(scores, axis=-1, keepdims=True)
            weights = jnp.where(live, jnp.exp(scores - top), 0.0).astype(BF16)
            total = jnp.sum(weights.astype(F32), axis=-1, keepdims=True)
            summed = lax.dot_general(
                weights, keys[:LATENT], (((1,), (1,)), ((), ())), preferred_element_type=F32
            )
            some = total > 0.0
            safe = jnp.where(some, total, 1.0)
            mean = summed / safe
            lse = jnp.where(some, top + jnp.log(safe), NEG_FILL)
            lse_all = jnp.where(column == r, lse, lse_all)
            for g in range(group):
                att_send[g, 16 * r : 16 * r + 16, :] = jnp.concatenate(
                    [mean[8 * g : 8 * g + 8], mean[heads + 8 * g : heads + 8 * g + 8]], axis=0
                ).astype(BF16)
        for g in range(group):
            lse_send[g] = jnp.concatenate(
                [lse_all[8 * g : 8 * g + 8], lse_all[heads + 8 * g : heads + 8 * g + 8]], axis=0
            )

    def attention_copies(k):
        to = lax.rem(my_g + k, group)
        return [
            pltpu.make_async_remote_copy(
                src_ref=a.at[to],
                dst_ref=b.at[k - 1],
                send_sem=att_s.at[n, k - 1],
                recv_sem=att_r.at[n, k - 1],
                device_id=device_of(to),
                device_id_type=MESH,
            )
            for n, (a, b) in enumerate(((att_send, att_got), (lse_send, lse_got)))
        ]

    def attention_send(ks):
        for k in ks:
            for copy in attention_copies(k):
                copy.start()

    def attention_finish():
        for k in range(1, group):
            for copy in attention_copies(k):
                copy.wait()
        for r in range(rows):
            tops = [lse_send[my_g][:, r : r + 1]]
            tops += [lse_got[k][:, r : r + 1] for k in range(group - 1)]
            best = functools.reduce(jnp.maximum, tops)
            factors = [jnp.exp(top - best) for top in tops]
            share = 1.0 / functools.reduce(jnp.add, factors)
            at = slice(16 * r, 16 * r + 16)
            total = att_send[my_g, at, :].astype(F32) * (factors[0] * share)
            for k in range(group - 1):
                total += att_got[k, at, :].astype(F32) * (factors[k + 1] * share)
            for t in range(LOOPS):
                att_out[t, r] = total[8 * t : 8 * t + 8].astype(BF16)


    def gather_copy(t, c, k):
        at = rows_all.at[t, c, cx, 0 : halves[c], :]
        return pltpu.make_async_remote_copy(
            src_ref=at, dst_ref=at, send_sem=ag_s.at[t, c, k - 1], recv_sem=ag_r.at[t, c, k - 1],
            device_id=(me, x_peer(k), cp), device_id_type=MESH,
        )

    def reduce_copy(t, c, k):
        return pltpu.make_async_remote_copy(
            src_ref=part.at[t, c, k, 0 : halves[c], :],
            dst_ref=red_got.at[t, c, k - 1, 0 : halves[c], :],
            send_sem=rs_s.at[t, c, k - 1], recv_sem=rs_r.at[t, c, k - 1],
            device_id=(me, x_peer(k), cp), device_id_type=MESH,
        )

    def weight_copies():
        places = (
            (w_gu.at[:, 0 : 2 * LANES], w_gu.at[:, 2 * LANES : 4 * LANES]),
            (w_down.at[0:LANES, :], w_down.at[LANES : 2 * LANES, :]),
        )
        return [
            pltpu.make_async_remote_copy(
                src_ref=a, dst_ref=b, send_sem=w_s.at[n], recv_sem=w_r.at[n],
                device_id=sibling, device_id_type=MESH,
            )
            for n, (a, b) in enumerate(places)
        ]

    def combine_copy(t, k):
        at = comb.at[t, my_g]
        return pltpu.make_async_remote_copy(
            src_ref=at, dst_ref=at,
            send_sem=comb_s.at[t, k - 1], recv_sem=comb_r.at[t, k - 1],
            device_id=(me, x_peer(k // 2), 1 - cp if k % 2 else cp), device_id_type=MESH,
        )

    near_first = [k for k in range(1, nx) if k in (1, nx - 1)]
    near_first += [k for k in range(1, nx) if k not in (1, nx - 1)]
    far_first = near_first[::-1]
    others = [n for k in far_first for n in (2 * k, 2 * k + 1)] + [1]

    def stage_a(t, c):
        at, half = spans[c], halves[c]
        wait_bytes(disp_got.at[t, at, :], disp_r.at[t, c])
        got = jnp.dot(
            order[c, : jb * half, : 8 * half], disp_got[t, at, :], preferred_element_type=F32
        ).astype(BF16)
        for j in range(jb):
            rows_all[t, c, cx, 0:half, j * LANES : (j + 1) * LANES] = got[half * j : half * j + half]
        for k in far_first:
            gather_copy(t, c, k).start()

    def stage_c(t, c):
        half = halves[c]
        total = jnp.zeros((half, 4 * LANES), F32)
        for k in [0] + near_first:
            if k:
                gather_copy(t, c, k).wait_recv()
            at = x_peer(nx - k) if k else cx
            total += jnp.dot(
                rows_all[t, c, at, :half, :],
                w_gu[pl.ds(pl.multiple_of(at * fx, LANES), fx), :],
                preferred_element_type=F32,
            )
        gate = jnp.concatenate([total[:, :LANES], total[:, 2 * LANES : 3 * LANES]], axis=1)
        up = jnp.concatenate([total[:, LANES : 2 * LANES], total[:, 3 * LANES :]], axis=1)
        active = (gate * (1.0 / (1.0 + jnp.exp(-gate))) * up).astype(BF16)
        for k in far_first + [0]:
            at = pl.multiple_of(x_peer(k) * fx, LANES)
            part[t, c, k, :half, :] = jnp.dot(
                active, w_down[:, pl.ds(at, fx)], preferred_element_type=F32
            ).astype(BF16)
            if k:
                reduce_copy(t, c, k).start()

    def stage_e(t, c):
        half = halves[c]
        summed = part[t, c, 0, :half, :].astype(F32)
        for k in near_first:
            reduce_copy(t, c, k).wait_recv()
            summed += red_got[t, c, k - 1, :half, :].astype(F32)
        for j in range(jb):
            stacked[half * j : half * j + half, :] = summed[:, j * LANES : (j + 1) * LANES].astype(BF16)
        back[t, spans[c], :] = jnp.dot(
            disorder[c, : 8 * half, : jb * half], stacked[: jb * half, :], preferred_element_type=F32
        ).astype(BF16)
        exchange(t, first[c + 1] - 1, CHUNKS[c], back, back_got, back_s, back_r, -1)

    stages = {"A": stage_a, "C": stage_c, "E": stage_e}

    dispatch_tiles(0)
    reorder_tables()
    for copy in loads[3:5]:
        copy.wait()
    attention_partials()
    for copy in loads[5:]:
        copy.wait()
    pl.semaphore_wait(barrier, ni - 1 + cp + group - 1)

    for t in range(LOOPS):
        exchange(t, ni - 1, ni, disp, disp_got, disp_s, disp_r, 1)
        attention_send([4, 3, 5] if t == 0 else [2, 6, 7])
        if t == 0:
            for copy in weight_copies():
                copy.start()
            for copy in weight_copies():
                copy.wait_recv()
        for step in PLAN:
            stages[step[0]](t, int(step[1:]))
        if t == 0:
            attention_send([1])
            route_tables(1)
        else:
            attention_finish()
            for copy in weight_copies():
                copy.wait_send()
            exchange_sent(0, back, back_s)
            for u in range(LOOPS):
                exchange_sent(u, disp, disp_s)
                for c in range(len(CHUNKS)):
                    for k in range(1, nx):
                        gather_copy(u, c, k).wait_send()
                        reduce_copy(u, c, k).wait_send()
            for k in range(1, group):
                combine_copy(0, k).wait_send()
        routed = jnp.zeros((LANES, LANES), F32)
        for c, at in enumerate(spans):
            wait_bytes(back_got.at[t, at, :], back_r.at[t, c])
            routed += jnp.dot(combine_t[t, :, at], back_got[t, at, :], preferred_element_type=F32)
        comb[t, my_g] = (routed[0:64] + routed[64:128]).astype(BF16)
        for k in others:
            combine_copy(t, k).start()
        for k in [0] + near_first:
            for n in (2 * k, 2 * k + 1):
                if n:
                    combine_copy(t, n).wait_recv()
            x = x_peer(nx - k) if k else cx
            pair = comb[t, 2 * x].astype(F32) + comb[t, 2 * x + 1].astype(F32)
            for j in range(jb):
                at = pl.ds(pl.multiple_of(x * fx + j * LANES, LANES), LANES)
                hidden[:, at] = (mixed[:, at] + pair[8 * j : 8 * j + 8]).astype(BF16).astype(F32)
        if t + 1 < LOOPS:
            dispatch_tiles(t + 1)
    hid_out[...] = hidden[0:rows, :].astype(BF16)

    exchange_sent(1, back, back_s)
    for k in range(1, group):
        combine_copy(1, k).wait_send()


def body(
    ne, nx,
    hidden_in, draft_embeds, norm_gains, queries, latent_cache, lengths, route_ids, route_weights,
    w_gate, w_up, w_down,
):
    rows, width = hidden_in.shape
    topk = route_ids.shape[2]
    fx = width // nx
    jb = fx // LANES
    ni = ne // 2
    nn = 16 * ni
    nc = len(CHUNKS)
    most = max(CHUNKS)
    half = 2 * most
    group = 2 * nx
    sizes = (ne, nx, rows, jb, topk, float(queries.shape[3]) ** (-0.5))
    hbm = pl.BlockSpec(memory_space=pltpu.HBM)
    vmem = pl.BlockSpec(memory_space=pltpu.VMEM)
    dma = pltpu.SemaphoreType.DMA
    scratch = [
        pltpu.SMEM(lengths.shape, jnp.int32),
        pltpu.SMEM((rows, LOOPS, topk), jnp.int32),
        pltpu.SMEM((rows, LOOPS, topk), F32),
        pltpu.VMEM(hidden_in.shape, BF16),
        pltpu.VMEM((rows, LOOPS, width), BF16),
        pltpu.VMEM(norm_gains.shape, F32),
        pltpu.VMEM(queries.shape, BF16),
        pltpu.VMEM((rows, latent_cache.shape[2], LANES), BF16),
        pltpu.VMEM((width, 4 * LANES), BF16),
        pltpu.VMEM((2 * LANES, width), BF16),
        pltpu.VMEM((8, width), F32),
        pltpu.VMEM((LOOPS, 8, width), F32),
        pltpu.VMEM((8, width), F32),
        pltpu.VMEM((LANES, LANES), F32),
        pltpu.VMEM((LOOPS, nn, LANES), BF16),
        pltpu.VMEM((LOOPS, LANES, nn), BF16),
        pltpu.VMEM((nc, jb * half, 16 * most), BF16),
        pltpu.VMEM((nc, 16 * most, jb * half), BF16),
        pltpu.VMEM((LOOPS, nn, LANES), BF16),
        pltpu.VMEM((LOOPS, nn, LANES), BF16),
        pltpu.VMEM((LOOPS, nc, nx, half, fx), BF16),
        pltpu.VMEM((LOOPS, nc, nx, half, fx), BF16),
        pltpu.VMEM((LOOPS, nc, nx - 1, half, fx), BF16),
        pltpu.VMEM((jb * half, LANES), BF16),
        pltpu.VMEM((LOOPS, nn, LANES), BF16),
        pltpu.VMEM((LOOPS, nn, LANES), BF16),
        pltpu.VMEM((LOOPS, group, 64, LANES), BF16),
        pltpu.VMEM((group, 16 * rows, LATENT), BF16),
        pltpu.VMEM((group - 1, 16 * rows, LATENT), BF16),
        pltpu.VMEM((group, 16, LANES), F32),
        pltpu.VMEM((group - 1, 16, LANES), F32),
        dma((3,)), dma((8,)), dma((2,)), dma((2,)),
        dma((LOOPS,)), dma((LOOPS, nc)),
        dma((LOOPS, nc, nx - 1)), dma((LOOPS, nc, nx - 1)),
        dma((LOOPS, nc, nx - 1)), dma((LOOPS, nc, nx - 1)),
        dma((LOOPS,)), dma((LOOPS, nc)),
        dma((LOOPS, group - 1)), dma((LOOPS, group - 1)),
        dma((2, group - 1)), dma((2, group - 1)),
    ]
    heads_here = queries.shape[2] // group
    return tuple(
        pl.pallas_call(
            functools.partial(kernel, sizes),
            out_shape=(
                jax.ShapeDtypeStruct((LOOPS, rows, heads_here, LATENT), BF16),
                jax.ShapeDtypeStruct((rows, width), BF16),
            ),
            in_specs=[hbm] * 11,
            out_specs=(vmem, vmem),
            scratch_shapes=scratch,
            compiler_params=pltpu.CompilerParams(
                collective_id=0, has_side_effects=True, vmem_limit_bytes=60 * 1024 * 1024
            ),
            name="draft_steps",
        )(
            hidden_in, jnp.swapaxes(draft_embeds, 0, 1), norm_gains, queries,
            jnp.swapaxes(latent_cache, 1, 2), lengths, jnp.swapaxes(route_ids, 0, 1),
            jnp.swapaxes(route_weights, 0, 1), w_gate[0], w_up[0], w_down[0],
        )
    )


def solution(mesh):
    in_specs = (
        P("expert", None),
        P(None, "expert", None),
        P(),
        P(None, "expert", None, None),
        P("expert", ("context", "pipe"), None),
        P("expert"),
        P(None, "expert", None),
        P(None, "expert", None),
        P("expert", None, ("context", "pipe")),
        P("expert", None, ("context", "pipe")),
        P("expert", ("context", "pipe"), None),
    )
    out_specs = (P(None, "expert", ("context", "pipe"), None), P("expert", None))
    run = functools.partial(body, mesh.shape["expert"], mesh.shape["context"])
    return jax.shard_map(run, mesh=mesh, in_specs=in_specs, out_specs=out_specs, check_vma=False)
```
